32 devices in a mesh: seq: 8 (over z, y), head: 4 (over x, core).
Axes of the slice: x: 2, y: 2, z: 4, core: 2. Of those that a mesh axis runs over, the one named last changes fastest.
Arguments:
- queries: bfloat16 [8192, 512], P('seq', 'head'), may hold values from -6 to 6
- keys: bfloat16 [8192, 512], P('seq', 'head'), may hold values from -6 to 6
- values: bfloat16 [8192, 512], P('seq', 'head'), may hold values from -6 to 6
- outputs: bfloat16 [8192, 512], P('seq', 'head'), may hold values from -6 to 6
- d_outputs: bfloat16 [8192, 512], P('seq', 'head'), may hold values from -6 to 6
- log_norm: float32 [8, 8192], P('head', 'seq'), may hold values from 4 to 5.5
- rand_owner: int32 [64, 3], P('seq'), may hold values from 0 to 7, all different within a row; in each aligned block of 8 rows (0 to 7, 8 to 15, ...) at most 3 rows name the same one
- rand_local: int32 [64, 3], P('seq'), may hold values from 0 to 7
- glob_blocks: int32 [2], replicated, may hold values from 0 to 63
Outputs:
- d_queries: bfloat16 [8192, 512], P('seq', 'head')
- d_keys: bfloat16 [8192, 512], P('seq', 'head')
- d_values: bfloat16 [8192, 512], P('seq', 'head')
The draws below stay inside these ranges and needn't reach their ends.
Inputs may be any that keep to these rules, and one draw needn't show every extreme that they name: `rand_owner`: each row names 3 different seq indices; within the 8 rows of one seq index no value is named more than 3 times, a bound that some block reaches.
All inputs are finite; a program needn't handle non-finite values.
Results may differ from the reference program's by a relative error of at most 0.0085.
Values may be sent and summed in bfloat16 or wider, within the bound.
No kernel may reach another device: no remote copies, remote signals or barrier semaphores. Data moves between devices by JAX's collectives and lax.ppermute only.
A program may use at most 128 MiB of HBM per device.

```python
import math
import jax
import jax.numpy as jnp
import numpy as np
from jax import lax

BLOCK = 128
DH = 64
HEADS = 8
G = 2
R = 3
QB_DEV = 8
NB = 64
TOKENS = 8192
RCAP = 3
N_SEQ = 8


def set_ends(result, rng, least, largest):
    index_at = [jax.random.randint(jax.random.fold_in(rng, axis), (), 0, length) for axis, length in enumerate(result.shape)]
    main_axis = result.shape.index(max(result.shape))
    next_to = index_at[:main_axis] + [(index_at[main_axis] + 1) % result.shape[main_axis]] + index_at[main_axis + 1:]
    return result.at[tuple(index_at)].set(least).at[tuple(next_to)].set(largest)


def levels(key, dims, cuts, low, top_value):
    level = 1.0
    for dim, shards_of in cuts:
        steps = jax.random.uniform(jax.random.fold_in(jax.random.fold_in(key, 6), dim), (shards_of,), jnp.float32, low / len(cuts), top_value / len(cuts))
        level = level * jnp.repeat(jnp.exp(steps), dims[dim] // shards_of).reshape((-1,) + (1,) * (len(dims) - 1 - dim))
    return level


def assign_block(own_key, own, number, rows, count, top, reach, slope):
    order = jax.random.permutation(own_key, count)
    packed, usual = portions_of(count, rows * top, reach, slope, True), portions_of(count, rows * top, reach, slope, False)
    places = jnp.arange(count)

    def named(sizes, turn):
        used = int((sizes > 0).sum())
        fixed = max(1, used // 4)
        shifted = fixed + (places - fixed + turn * (used - fixed)) % max(1, count - fixed)
        return jnp.zeros((count,), jnp.int32).at[order[jnp.where(places < fixed, places, shifted)]].set(jnp.asarray(sizes, jnp.int32))

    sizes = jnp.where(number % 4 == 0, named(packed, number // 4), named(usual, number - number // 4 - 1))
    mixed = jax.random.permutation(jax.random.fold_in(own, 3), count)
    source_of, taker = mixed[0:count // 2 * 2:2], mixed[1:count // 2 * 2:2]
    slack = jnp.minimum(sizes[source_of] - 1, reach - sizes[taker]) // 2
    slack = jnp.where((source_of == order[0]) | (taker == order[0]) | (sizes[taker] == 0), 0, jnp.maximum(slack, 0))
    shifted = jax.random.randint(jax.random.fold_in(own, 4), (count // 2,), 0, 1 << 20) % (slack + 1)
    sizes = sizes.at[source_of].add(-shifted).at[taker].add(shifted)
    members = jnp.searchsorted(jnp.cumsum(sizes), jnp.arange(rows * top), side="right").astype(jnp.int32)
    grid = members.reshape(top, rows).T
    grid = grid[jax.random.permutation(jax.random.fold_in(own, 1), rows)]
    turn = jax.random.randint(jax.random.fold_in(own, 2), (rows, 1), 0, top)
    return jnp.take_along_axis(grid, (jnp.arange(top)[None, :] + turn) % top, axis=1)


def portions_of(count, total, bound, slope, full):
    portions = [(1 << 20) // math.isqrt(standing ** slope) + 1 for standing in range(1, count + 1)]
    largest = bound if full else min(bound, max(-(-total // count), total * portions[0] // sum(portions)))
    least = 1 if total - largest >= count - 1 else 0
    holding, surplus = [largest] + [least] * (count - 1), total - largest - least * (count - 1)
    while surplus > 0:
        movable = [i for i in range(1, count) if holding[i] < largest] or [i for i in range(1, count) if holding[i] < bound]
        whole, budget = sum([portions[i] for i in movable]), surplus
        for i in movable:
            more = min(bound - holding[i], max(1, budget * portions[i] // whole), surplus)
            holding[i] = holding[i] + more
            surplus = surplus - more
    return np.array(holding)


def gaussian(stream_key, extent, spread, bound, split=(), kind=jnp.bfloat16):
    level = levels(stream_key, extent, split, -0.22, 0.18) if split else 1.0
    drawn = jax.random.normal(stream_key, extent, jnp.float32) * spread * level
    return jnp.minimum(jnp.maximum(drawn, -bound), bound).astype(kind)


def setup_inputs(seed: int = 0) -> dict:
    key_of = jax.random.split(jax.random.key(seed), 10)
    queries = gaussian(key_of[0], (TOKENS, HEADS * DH), 1.0, 6.0, ((0, 8), (1, 4)))
    keys = gaussian(key_of[1], (TOKENS, HEADS * DH), 1.0, 6.0, ((0, 8), (1, 4)))
    values = gaussian(key_of[2], (TOKENS, HEADS * DH), 1.0, 6.0, ((0, 8), (1, 4)))
    outputs = gaussian(key_of[3], (TOKENS, HEADS * DH), 1.0, 6.0, ((0, 8), (1, 4)))
    d_outputs = gaussian(key_of[4], (TOKENS, HEADS * DH), 1.0, 6.0, ((0, 8), (1, 4)))
    log_norm = jnp.clip(4.0 + 1.5 * jax.random.uniform(key_of[5], (HEADS, TOKENS), jnp.float32) ** levels(key_of[5], (HEADS, TOKENS), ((0, 4), (1, 8)), -0.2, 0.2), 4.0, 5.5)
    rand_owner_keys = jax.random.split(jax.random.fold_in(key_of[6], 1), NB // QB_DEV)
    rand_owner_turns = jax.random.permutation(jax.random.fold_in(key_of[6], 3), NB // QB_DEV)
    rand_owner = jax.vmap(lambda own, number: assign_block(jax.random.fold_in(key_of[6], 2), own, number, QB_DEV, N_SEQ, R, RCAP, 2))(rand_owner_keys, rand_owner_turns).reshape((NB, R))
    rand_local = set_ends(jax.random.randint(key_of[7], (NB, R), 0, QB_DEV), jax.random.fold_in(key_of[7], 1), 0, QB_DEV - 1).astype(jnp.int32)
    glob_blocks = jax.random.randint(key_of[8], (G,), 0, NB).astype(jnp.int32)
    return {"queries": queries, "keys": keys, "values": values, "outputs": outputs, "d_outputs": d_outputs, "log_norm": log_norm, "rand_owner": rand_owner, "rand_local": rand_local, "glob_blocks": glob_blocks}


def rounded(value):
    return lax.optimization_barrier(value.astype(jnp.bfloat16)).astype(jnp.float32)

def reference(queries, keys, values, outputs, d_outputs, log_norm, rand_owner, rand_local, glob_blocks):
    factor = 1.0 / math.sqrt(DH)
    blocks = TOKENS // BLOCK
    block_shape = (blocks, BLOCK, HEADS, DH)
    query_all = queries.astype(jnp.float32).reshape(block_shape)
    key_all = keys.astype(jnp.float32).reshape(block_shape)
    value_all = values.astype(jnp.float32).reshape(block_shape)
    output_all = outputs.astype(jnp.float32).reshape(block_shape)
    grad_all = d_outputs.astype(jnp.float32).reshape(block_shape)
    delta_all = lax.optimization_barrier(jnp.sum(output_all * grad_all, axis=-1)).transpose(0, 2, 1)
    norm_all = log_norm.reshape(HEADS, blocks, BLOCK).transpose(1, 0, 2)
    border = jnp.zeros((1, BLOCK, HEADS, DH), jnp.float32)
    keys_pad = jnp.concatenate([border, key_all, border], axis=0)
    values_pad = jnp.concatenate([border, value_all, border], axis=0)
    block_ids = jnp.arange(blocks, dtype=jnp.int32)
    window = block_ids[:, None] + jnp.arange(3, dtype=jnp.int32)[None, :]
    global_ids = jnp.broadcast_to(glob_blocks.astype(jnp.int32)[None, :] + 1, (blocks, G))
    randoms = (rand_owner * QB_DEV + rand_local + 1).astype(jnp.int32)
    listing = jnp.concatenate([window, global_ids, randoms], axis=1).astype(jnp.int32)
    groups = blocks // QB_DEV

    def regroup(array):
        return array.reshape((groups, QB_DEV) + array.shape[1:])

    def group_step(running, slices):
        acc_keys, acc_values = running
        query_rows, grad_rows, norm_rows, delta_rows, ids_rows = slices
        key_rows = keys_pad[ids_rows]
        value_rows = values_pad[ids_rows]
        scores = jnp.einsum('nqhd,nmkhd->nmhqk', query_rows, key_rows) * factor
        weights = jnp.exp(scores - norm_rows[:, None, :, :, None])
        grad_weights = jnp.einsum('nqhd,nmkhd->nmhqk', grad_rows, value_rows)
        grad_scores = weights * (grad_weights - delta_rows[:, None, :, :, None])
        weights_low = rounded(weights)
        scores_low = rounded(grad_scores)
        grad_query = jnp.einsum('nmhqk,nmkhd->nqhd', scores_low, key_rows) * factor
        grad_key = jnp.einsum('nmhqk,nqhd->nmkhd', scores_low, query_rows) * factor
        grad_value = jnp.einsum('nmhqk,nqhd->nmkhd', weights_low, grad_rows)
        flat_ids = ids_rows.reshape(-1)
        acc_keys = acc_keys.at[flat_ids].add(grad_key.reshape((-1, BLOCK, HEADS, DH)))
        acc_values = acc_values.at[flat_ids].add(grad_value.reshape((-1, BLOCK, HEADS, DH)))
        return ((acc_keys, acc_values), grad_query)
    empty_acc = jnp.zeros((blocks + 2, BLOCK, HEADS, DH), jnp.float32)
    (acc_keys, acc_values), grad_queries = lax.scan(group_step, (empty_acc, empty_acc), (regroup(query_all), regroup(grad_all), regroup(norm_all), regroup(delta_all), regroup(listing)))
    features = HEADS * DH
    d_queries = grad_queries.reshape(TOKENS, features).astype(jnp.bfloat16)
    d_keys = acc_keys[1:-1].reshape(TOKENS, features).astype(jnp.bfloat16)
    d_values = acc_values[1:-1].reshape(TOKENS, features).astype(jnp.bfloat16)
    return (d_queries, d_keys, d_values)
```

```python
import functools
import math

import jax
import jax.numpy as jnp
from jax import lax
from jax.experimental import pallas as pl
from jax.experimental.pallas import tpu as pltpu
from jax.sharding import PartitionSpec as P

BLOCK = 128
STAT = 8
LOG2E = math.log2(math.e)
NT = (((1,), (1,)), ((), ()))
VMEM = pl.BlockSpec(memory_space=pltpu.VMEM)
SMEM = pl.BlockSpec(memory_space=pltpu.SMEM)
F32 = jnp.float32
BF16 = jnp.bfloat16


def call(body, out_shape, out_specs, in_specs, scratch, flops, moved, name):
    return pl.pallas_call(
        body,
        out_shape=out_shape,
        in_specs=in_specs,
        out_specs=out_specs,
        scratch_shapes=scratch,
        compiler_params=pltpu.CompilerParams(vmem_limit_bytes=48 * 1024 * 1024),
        cost_estimate=pl.CostEstimate(flops=flops, bytes_accessed=moved, transcendentals=0),
        name=name,
    )


def dot(a, b):
    return jnp.dot(a, b, preferred_element_type=F32)


def by_head(rows, heads):
    width = rows.shape[1] // heads
    lane = lax.broadcasted_iota(jnp.int32, (1, rows.shape[1]), 1)
    parts = []
    for h in range(heads):
        keep = ((lane >= h * width) & (lane < (h + 1) * width)).astype(F32).astype(BF16)
        parts.append(rows * keep)
    return jnp.concatenate(parts, axis=0)


def stat_rows(tile, heads):
    half = 2 * heads
    norm = [tile[h : h + 1] + tile[heads + h : heads + h + 1] for h in range(heads)]
    delta = [tile[half + h : half + h + 1] + tile[half + heads + h : half + heads + h + 1] for h in range(heads)]
    return jnp.concatenate(norm, axis=1), jnp.concatenate(delta, axis=1)


def weigh(key_rows, value_rows, q_bd, g_bd, norm, delta):
    scores = lax.dot_general(key_rows, q_bd, NT, preferred_element_type=F32)
    weights = jnp.exp2(scores * LOG2E - norm)
    grad = lax.dot_general(value_rows, g_bd, NT, preferred_element_type=F32)
    return weights.astype(BF16), (weights * (grad - delta)).astype(BF16)


def grad_query_t(keys_t, low, heads):
    width = keys_t.shape[0] // heads
    return jnp.concatenate(
        [dot(keys_t[h * width : (h + 1) * width], low[:, h * BLOCK : (h + 1) * BLOCK]) for h in range(heads)],
        axis=0,
    )


def pack_queries(heads, per_block, capacity, fold, refs):
    (q_ref, g_ref, o_ref, norm_ref, owner_ref, local_ref, scale_q_ref, stats_ref, src_ref) = refs[:9]
    out_refs, (count, source, place) = refs[9:-3], refs[-3:]
    blocks = q_ref.shape[0] // BLOCK
    owners = len(out_refs)
    width = q_ref.shape[1] // heads
    me = lax.axis_index("seq") if fold else 0
    for k in range(owners):
        count[k] = 0
        for s in range(capacity):
            source[k * capacity + s] = -1
    for b in range(blocks):
        for r in range(per_block):
            k = owner_ref[b, r] ^ me
            s = count[k]
            count[k] = s + 1
            source[k * capacity + s] = b
            place[k * capacity + s] = local_ref[b, r]
    for b in range(blocks):
        rows = pl.ds(b * BLOCK, BLOCK)
        prod = (o_ref[rows, :].astype(F32) * g_ref[rows, :].astype(F32)).T
        norm = [norm_ref[h : h + 1, rows] * LOG2E for h in range(heads)]
        delta = [jnp.sum(prod[h * width : (h + 1) * width], axis=0, keepdims=True) for h in range(heads)]
        exact = jnp.concatenate(norm + delta, axis=0)
        high = exact.astype(BF16).astype(F32)
        low = (exact - high).astype(BF16).astype(F32)
        stats_ref[b] = jnp.concatenate(
            [high[:heads], low[:heads], high[heads:], low[heads:]], axis=0
        )
        scale_q_ref[rows, :] = q_ref[rows, :] * jnp.asarray(1.0 / math.sqrt(width), BF16)
    full = blocks * per_block == owners * capacity
    for k in range(owners):
        out = out_refs[k]
        tiles, marks = [], []
        for s in range(capacity):
            b = source[k * capacity + s]
            src_ref[k * capacity + s] = b
            at = pl.ds(pl.multiple_of(jnp.maximum(b, 0) * BLOCK, BLOCK), BLOCK)
            query, grad, tile = scale_q_ref[at, :], g_ref[at, :], stats_ref[jnp.maximum(b, 0)]
            number = place[k * capacity + s]
            if not full:
                query = jnp.where(b >= 0, query, jnp.zeros_like(query))
                grad = jnp.where(b >= 0, grad, jnp.zeros_like(grad))
                tile = jnp.where(b >= 0, tile, jnp.zeros_like(tile))
                number = jnp.where(b >= 0, number, 0)
            out[2 * s * BLOCK : (2 * s + 1) * BLOCK, :] = query
            out[(2 * s + 1) * BLOCK : (2 * s + 2) * BLOCK, :] = grad
            tiles.append(tile)
            marks.append(jnp.full((1, BLOCK), number, jnp.int32).astype(F32))
        extra = out.shape[0] - (2 * BLOCK + STAT) * capacity - capacity
        marks.append(jnp.zeros((extra, BLOCK), F32))
        out[2 * capacity * BLOCK :, :] = jnp.concatenate(tiles + marks, axis=0).astype(BF16)


def pack_keys(head_size, k_ref, v_ref, q_ref, g_ref, stats_ref, glob_ref, up_ref, down_ref, own_ref, kt_ref):
    blocks = k_ref.shape[0] // BLOCK
    me = lax.axis_index("seq")
    for out, b in ((up_ref, blocks - 1), (down_ref, 0)):
        rows = pl.ds(b * BLOCK, BLOCK)
        for number, ref in enumerate((q_ref, g_ref, k_ref, v_ref)):
            out[number * BLOCK : (number + 1) * BLOCK, :] = ref[rows, :]
        out[4 * BLOCK :, :] = jnp.concatenate(
            [stats_ref[b], jnp.zeros((STAT, BLOCK), F32)], axis=0
        ).astype(BF16)
    for number in range(glob_ref.shape[0]):
        block = glob_ref[number]
        mine = block // blocks == me
        at = pl.ds(pl.multiple_of((block % blocks) * BLOCK, BLOCK), BLOCK)
        for turn, ref in enumerate((k_ref, v_ref)):
            first = (turn * glob_ref.shape[0] + number) * BLOCK
            rows = ref[at, :]
            own_ref[first : first + BLOCK, :] = jnp.where(mine, rows, jnp.zeros_like(rows))
    for b in range(blocks):
        rows = pl.ds(b * BLOCK, BLOCK)
        kt_ref[rows, :] = (k_ref[rows, :].astype(F32) * (1.0 / math.sqrt(head_size))).T.astype(BF16)


def window(
    heads, q_ref, g_ref, stats_ref, k_ref, v_ref, kt_ref, before_ref, after_ref, dqt_ref, dk_ref, dv_ref
):
    blocks = q_ref.shape[0] // BLOCK
    head_size = q_ref.shape[1] // heads

    def piece(ref, number):
        return ref[number * BLOCK : (number + 1) * BLOCK, :]

    def edge_t(ref):
        return (piece(ref, 2).astype(F32) * (1.0 / math.sqrt(head_size))).T.astype(BF16)

    def key_side(j):
        if j < 0:
            return piece(before_ref, 2), piece(before_ref, 3), edge_t(before_ref)
        if j == blocks:
            return piece(after_ref, 2), piece(after_ref, 3), edge_t(after_ref)
        return piece(k_ref, j), piece(v_ref, j), piece(kt_ref, j)

    for b in range(-1, blocks + 1):
        inside = 0 <= b < blocks
        if inside:
            query, grad, tile = piece(q_ref, b), piece(g_ref, b), stats_ref[b]
        else:
            ref = before_ref if b < 0 else after_ref
            query, grad, tile = piece(ref, 0), piece(ref, 1), ref[4 * BLOCK :, :].astype(F32)[:STAT]
        q_bd, g_bd = by_head(query, heads), by_head(grad, heads)
        norm, delta = stat_rows(tile, heads)
        near = range(b - 1, b + 2) if inside else [0 if b < 0 else blocks - 1]
        total = None
        for j in near:
            key_rows, value_rows, keys_t = key_side(j)
            weights_low, scores_low = weigh(key_rows, value_rows, q_bd, g_bd, norm, delta)
            if inside:
                term = grad_query_t(keys_t, scores_low, heads)
                total = term if total is None else total + term
            if 0 <= j < blocks:
                rows = pl.ds(j * BLOCK, BLOCK)
                grad_key, grad_value = dot(scores_low, q_bd), dot(weights_low, g_bd)
                if b == j - 1:
                    dk_ref[rows, :] = grad_key
                    dv_ref[rows, :] = grad_value
                else:
                    dk_ref[rows, :] += grad_key
                    dv_ref[rows, :] += grad_value
        if inside:
            dqt_ref[b * BLOCK : (b + 1) * BLOCK, :] = total


def globals_(heads, q_ref, g_ref, stats_ref, shared_ref, before_ref, dqt_ref, part_ref, total_k, total_v):
    blocks = q_ref.shape[0] // BLOCK
    head_size = q_ref.shape[1] // heads
    rows = shared_ref.shape[0] // 2
    key_rows, value_rows = shared_ref[:rows, :], shared_ref[rows:, :]
    keys_t = (key_rows.astype(F32) * (1.0 / math.sqrt(head_size))).T.astype(BF16)
    for b in range(blocks):
        at = pl.ds(b * BLOCK, BLOCK)
        q_bd, g_bd = by_head(q_ref[at, :], heads), by_head(g_ref[at, :], heads)
        norm, delta = stat_rows(stats_ref[b], heads)
        weights_low, scores_low = weigh(key_rows, value_rows, q_bd, g_bd, norm, delta)
        dqt_ref[at, :] = before_ref[at, :] + grad_query_t(keys_t, scores_low, heads)
        grad_key, grad_value = dot(scores_low, q_bd), dot(weights_low, g_bd)
        if b == 0:
            total_k[...] = grad_key
            total_v[...] = grad_value
        else:
            total_k[...] += grad_key
            total_v[...] += grad_value
    part_ref[:rows, :] = total_k[...].astype(BF16)
    part_ref[rows:, :] = total_v[...].astype(BF16)


def randoms(heads, capacity, in_ref, k_ref, v_ref, kt_ref, dk_in, dv_in, ret_ref, dk_ref, dv_ref):
    dk_ref[...] = dk_in[...]
    dv_ref[...] = dv_in[...]

    def partner(n):
        tail = in_ref[n, 2 * capacity * BLOCK :, :].astype(F32)
        for s in range(capacity):
            mark = STAT * capacity + s
            number = jnp.max(tail[mark : mark + 1]).astype(jnp.int32)
            at = pl.ds(pl.multiple_of(number * BLOCK, BLOCK), BLOCK)
            query = in_ref[n, 2 * s * BLOCK : (2 * s + 1) * BLOCK, :]
            grad = in_ref[n, (2 * s + 1) * BLOCK : (2 * s + 2) * BLOCK, :]
            q_bd, g_bd = by_head(query, heads), by_head(grad, heads)
            norm, delta = stat_rows(tail[s * STAT : (s + 1) * STAT], heads)
            weights_low, scores_low = weigh(k_ref[at, :], v_ref[at, :], q_bd, g_bd, norm, delta)
            ret_ref[n, s * BLOCK : (s + 1) * BLOCK, :] = grad_query_t(kt_ref[at, :], scores_low, heads).astype(BF16)
            dk_ref[at, :] += dot(scores_low, q_bd)
            dv_ref[at, :] += dot(weights_low, g_bd)

    if in_ref.shape[0] == 1:
        partner(0)
    else:
        pl.loop(0, in_ref.shape[0])(partner)


def finish_keys(dk_in, dv_in, total_ref, glob_ref, dk_ref, dv_ref, sum_k, sum_v):
    blocks = dk_in.shape[0] // BLOCK
    me = lax.axis_index("seq")
    many = glob_ref.shape[0]
    sum_k[...] = dk_in[...]
    sum_v[...] = dv_in[...]
    for number in range(many):
        block = glob_ref[number]

        @pl.when(block // blocks == me)
        def _():
            at = pl.ds(pl.multiple_of((block % blocks) * BLOCK, BLOCK), BLOCK)
            for turn, ref in enumerate((sum_k, sum_v)):
                first = (turn * many + number) * BLOCK
                ref[at, :] += total_ref[first : first + BLOCK, :].astype(F32)

    dk_ref[...] = sum_k[...].astype(BF16)
    dv_ref[...] = sum_v[...].astype(BF16)


def finish_queries(capacity, refs):
    dqt_ref, src_ref, ret_refs, (out_ref, total) = refs[0], refs[1], refs[2:-2], refs[-2:]
    blocks = dqt_ref.shape[0] // BLOCK
    total[...] = dqt_ref[...]
    at = 0
    for ref in ret_refs:
        for n in range(ref.shape[0]):
            for s in range(capacity):
                b = src_ref[at]
                at += 1

                @pl.when(b >= 0)
                def _():
                    rows = pl.ds(pl.multiple_of(b * BLOCK, BLOCK), BLOCK)
                    total[rows, :] += ref[n, s * BLOCK : (s + 1) * BLOCK, :].astype(F32)

    for b in range(blocks):
        rows = pl.ds(b * BLOCK, BLOCK)
        out_ref[rows, :] = total[rows, :].T.astype(BF16)


def shards(
    queries, keys, values, outputs, d_outputs, log_norm, rand_owner, rand_local, glob_blocks
):
    tokens, features = queries.shape
    heads = log_norm.shape[0]
    head_size = features // heads
    blocks = tokens // BLOCK
    per_block = rand_owner.shape[1]
    many = glob_blocks.shape[0]
    owners = lax.axis_size("seq")
    references = blocks * per_block
    capacity = max(2, (references + owners - 1) // owners)
    by_permute = owners <= 8
    rows = -(-((2 * BLOCK + STAT) * capacity + capacity) // 16) * 16
    whole = jax.ShapeDtypeStruct((tokens, features), BF16)
    wide = jax.ShapeDtypeStruct((tokens, features), F32)
    pair_flops = 10 * BLOCK * BLOCK * 256

    packed = call(
        lambda *refs: pack_queries(heads, per_block, capacity, by_permute, refs),
        [
            whole,
            jax.ShapeDtypeStruct((blocks, STAT, BLOCK), F32),
            jax.ShapeDtypeStruct((owners * capacity,), jnp.int32),
        ]
        + [jax.ShapeDtypeStruct((rows, features), BF16)] * owners,
        [VMEM, VMEM, SMEM] + [VMEM] * owners,
        [VMEM, VMEM, VMEM, VMEM, SMEM, SMEM],
        [
            pltpu.SMEM((owners,), jnp.int32),
            pltpu.SMEM((owners * capacity,), jnp.int32),
            pltpu.SMEM((owners * capacity,), jnp.int32),
        ],
        1 << 20,
        owners * rows * 256,
        "pack_queries",
    )(queries, d_outputs, outputs, log_norm, rand_owner, rand_local)
    scaled, stats, source = packed[:3]
    outgoing = packed[3:]

    def swap(array, k):
        return lax.ppermute(array, "seq", [(i, i ^ k) for i in range(owners)])

    if by_permute:
        order = sorted(range(1, owners), key=lambda k: (-(k & -2 & (owners // 2)), k))
        arrived = {k: swap(outgoing[k], k)[None] for k in order}
        arrived[0] = outgoing[0][None]
    else:
        everyone = lax.all_to_all(jnp.stack(outgoing), "seq", split_axis=0, concat_axis=0, tiled=True)

    edge = jax.ShapeDtypeStruct((4 * BLOCK + 16, features), BF16)
    up, down, own, keys_t = call(
        functools.partial(pack_keys, head_size),
        [edge, edge, jax.ShapeDtypeStruct((2 * many * BLOCK, features), BF16), whole],
        [VMEM] * 4,
        [VMEM] * 5 + [SMEM],
        [],
        1 << 20,
        tokens * features * 10,
        "pack_keys",
    )(keys, values, scaled, d_outputs, stats, glob_blocks)
    forward = [(i, i + 1) for i in range(owners - 1)]
    before = lax.ppermute(up, "seq", forward)
    after = lax.ppermute(down, "seq", [(j, i) for i, j in forward])

    shared = own
    step = 1
    while step < owners:
        shared = shared + swap(shared, step)
        step *= 2

    dqt, dk, dv = call(
        functools.partial(window, heads),
        [wide] * 3,
        [VMEM] * 3,
        [VMEM] * 8,
        [],
        3 * blocks * pair_flops,
        tokens * features * 24,
        "window",
    )(scaled, d_outputs, stats, keys, values, keys_t, before, after)

    def owned(taken, dk, dv):
        return call(
            functools.partial(randoms, heads, capacity),
            [jax.ShapeDtypeStruct((taken.shape[0], capacity * BLOCK, features), BF16), wide, wide],
            [VMEM] * 3,
            [VMEM] * 6,
            [],
            taken.shape[0] * capacity * pair_flops,
            tokens * features * 20,
            "randoms",
        )(taken, keys, values, keys_t, dk, dv)

    returned = {}
    if by_permute:
        returned[0], dk, dv = owned(arrived[0], dk, dv)
    dqt, part = call(
        functools.partial(globals_, heads),
        [wide, jax.ShapeDtypeStruct(own.shape, BF16)],
        [VMEM] * 2,
        [VMEM] * 5,
        [pltpu.VMEM((many * BLOCK, features), F32)] * 2,
        many * blocks * pair_flops,
        tokens * features * 16,
        "globals",
    )(scaled, d_outputs, stats, shared, dqt)
    step = 1
    while step < owners:
        part = (part.astype(F32) + swap(part, step).astype(F32)).astype(BF16)
        step *= 2

    if by_permute:
        for k in order:
            back, dk, dv = owned(arrived[k], dk, dv)
            returned[k] = swap(back, k)
        rets = [returned[k] for k in range(owners)]
    else:
        back, dk, dv = owned(everyone, dk, dv)
        rets = [lax.all_to_all(back, "seq", split_axis=0, concat_axis=0, tiled=True)]

    d_keys, d_values = call(
        finish_keys,
        [whole, whole],
        [VMEM] * 2,
        [VMEM] * 3 + [SMEM],
        [pltpu.VMEM((tokens, features), F32)] * 2,
        1 << 20,
        tokens * features * 12,
        "finish_keys",
    )(dk, dv, part, glob_blocks)
    d_queries = call(
        lambda *refs: finish_queries(capacity, refs),
        whole,
        VMEM,
        [VMEM, SMEM] + [VMEM] * len(rets),
        [pltpu.VMEM((tokens, features), F32)],
        1 << 20,
        tokens * features * 12,
        "finish_queries",
    )(dqt, source, *rets)
    return d_queries, d_keys, d_values


def solution(mesh):
    placed = (
        P("seq", "head"),
        P("seq", "head"),
        P("seq", "head"),
        P("seq", "head"),
        P("seq", "head"),
        P("head", "seq"),
        P("seq", None),
        P("seq", None),
        P(),
    )
    return jax.shard_map(
        shards,
        mesh=mesh,
        in_specs=placed,
        out_specs=(P("seq", "head"), P("seq", "head"), P("seq", "head")),
        check_vma=False,
    )
```

```python
import functools
import math

import jax
import jax.numpy as jnp
from jax import lax
from jax.experimental import pallas as pl
from jax.experimental.pallas import tpu as pltpu
from jax.sharding import PartitionSpec as P

BLOCK = 128
STAT = 8
LOG2E = math.log2(math.e)
NT = (((1,), (1,)), ((), ()))
VMEM = pl.BlockSpec(memory_space=pltpu.VMEM)
SMEM = pl.BlockSpec(memory_space=pltpu.SMEM)
HBM = pl.BlockSpec(memory_space=pltpu.HBM)
F32 = jnp.float32
BF16 = jnp.bfloat16
LIMIT = 24
PIECES = 4
COSTS = {'window': 3, 'randoms': 3, 'finish_keys': 3, 'finish_queries': 3}
GATES = {'W': ['G1'], 'F5': ['G1'], 'F6': ['G2', 'R0'], 'F7': ['F4'], 'F2': ['F5'], 'F3': ['F5'], 'R1': ['G2'], 'R3': ['R1'], 'r6': ['r4'], 'r7': ['r5'], 'P2': ['F6', 'F7', 'r4'], 'P3': ['r5', 'F5'], 'r1': ['r6']}
GROUPS = [[4], [0], [5], [1], [2], [6], [7], [3]]
HOPS = {'G': [4, 2, 1], 'P': [1, 2, 4]}


def call(body, out_shape, out_specs, in_specs, scratch, name, aliases={}, limit=24):
    return pl.pallas_call(
        body,
        out_shape=out_shape,
        in_specs=in_specs,
        out_specs=out_specs,
        scratch_shapes=scratch,
        input_output_aliases=aliases,
        compiler_params=pltpu.CompilerParams(vmem_limit_bytes=int(limit * 1024 * 1024)),
        cost_estimate=pl.CostEstimate(
            flops=int(COSTS.get(name, 0) * 1.15e9), bytes_accessed=0, transcendentals=0
        ),
        name=name,
    )


def after(array, *others):
    return lax.optimization_barrier((array, *others))[0] if others else array


def dot(a, b):
    return jnp.dot(a, b, preferred_element_type=F32)


def by_head(rows, heads):
    width = rows.shape[1] // heads
    lane = lax.broadcasted_iota(jnp.int32, (1, rows.shape[1]), 1)
    parts = []
    for h in range(heads):
        keep = ((lane >= h * width) & (lane < (h + 1) * width)).astype(F32).astype(BF16)
        parts.append(rows * keep)
    return jnp.concatenate(parts, axis=0)


def stat_rows(tile, heads):
    half = 2 * heads
    norm = [tile[h : h + 1] + tile[heads + h : heads + h + 1] for h in range(heads)]
    delta = [tile[half + h : half + h + 1] + tile[half + heads + h : half + heads + h + 1] for h in range(heads)]
    return jnp.concatenate(norm, axis=1), jnp.concatenate(delta, axis=1)


def weigh(key_rows, value_rows, q_bd, g_bd, norm, delta):
    scores = lax.dot_general(key_rows, q_bd, NT, preferred_element_type=F32)
    weights = jnp.exp2(scores * LOG2E - norm)
    grad = lax.dot_general(value_rows, g_bd, NT, preferred_element_type=F32)
    return weights.astype(BF16), (weights * (grad - delta)).astype(BF16)


def grad_query_t(keys_t, low, heads):
    width = keys_t.shape[0] // heads
    return jnp.concatenate(
        [dot(keys_t[h * width : (h + 1) * width], low[:, h * BLOCK : (h + 1) * BLOCK]) for h in range(heads)],
        axis=0,
    )


def message_rows(slots):
    return -(-((2 * BLOCK + STAT + 1) * slots) // 16) * 16


def pack(heads, plan, refs):
    q_hbm, g_hbm, o_hbm, k_hbm, v_hbm, norm_hbm, owner_ref, local_ref, glob_ref = refs[:9]
    scaled_ref, stats_ref, own_ref, kt_ref, src_ref = refs[9:14]
    out_refs = refs[14 : 14 + len(plan)]
    q_ref, g_ref, o_ref, k_ref, v_ref, norm_ref, sems, count, source, place = refs[14 + len(plan) :]
    copies = [
        pltpu.make_async_copy(a, b, sems.at[n])
        for n, (a, b) in enumerate(
            (
                (g_hbm, g_ref),
                (o_hbm, o_ref),
                (norm_hbm, norm_ref),
                (q_hbm, q_ref),
                (k_hbm, k_ref),
                (v_hbm, v_ref),
            )
        )
    ]
    for copy in copies:
        copy.start()
    blocks = q_ref.shape[0] // BLOCK
    per_block = owner_ref.shape[0]
    width = q_ref.shape[1] // heads
    me = lax.axis_index("seq")
    fold = any(entry[1] == "xor" for entry in plan)
    most = max(entry[0] for entry in plan)
    randoms = sum(1 for entry in plan if entry[0])
    for k in range(randoms):
        count[k] = 0
        for s in range(most):
            source[k * most + s] = -1
    for b in range(blocks):
        for r in range(per_block):
            k = owner_ref[r, b]
            if fold:
                k = k ^ me
            s = count[k]
            count[k] = s + 1
            source[k * most + s] = b
            place[k * most + s] = local_ref[r, b]
    for copy in copies[:3]:
        copy.wait()
    for b in range(blocks):
        rows = pl.ds(b * BLOCK, BLOCK)
        prod = (o_ref[rows, :].astype(F32) * g_ref[rows, :].astype(F32)).T
        norm = [norm_ref[h : h + 1, rows] * LOG2E for h in range(heads)]
        delta = [jnp.sum(prod[h * width : (h + 1) * width], axis=0, keepdims=True) for h in range(heads)]
        exact = jnp.concatenate(norm + delta, axis=0)
        high = exact.astype(BF16).astype(F32)
        low = (exact - high).astype(BF16).astype(F32)
        stats_ref[b] = jnp.concatenate([high[:heads], low[:heads], high[heads:], low[heads:]], axis=0)
    copies[3].wait()
    scaled_ref[...] = q_ref[...] * jnp.asarray(1.0 / math.sqrt(width), BF16)
    full = blocks * per_block == randoms * most
    done = 0
    for k, (slots, edge) in enumerate(plan):
        out = out_refs[k]
        tiles, marks = [], []
        total = slots + (edge not in (None, "xor"))
        for s in range(total):
            if s < slots:
                b, number, sure = source[k * most + s], place[k * most + s], full
            else:
                up, down = edge(me)
                b = jnp.where(up, blocks - 1, jnp.where(down, 0, -1))
                number, sure = jnp.where(up, 0, blocks - 1), False
            src_ref[done + s] = b
            safe = jnp.maximum(b, 0)
            at = pl.ds(pl.multiple_of(safe * BLOCK, BLOCK), BLOCK)
            query, grad, tile = scaled_ref[at, :], g_ref[at, :], stats_ref[safe]
            if not sure:
                query = jnp.where(b >= 0, query, jnp.zeros_like(query))
                grad = jnp.where(b >= 0, grad, jnp.zeros_like(grad))
                tile = jnp.where(b >= 0, tile, jnp.zeros_like(tile))
                number = jnp.where(b >= 0, number, 0)
            out[2 * s * BLOCK : (2 * s + 1) * BLOCK, :] = query
            out[(2 * s + 1) * BLOCK : (2 * s + 2) * BLOCK, :] = grad
            tiles.append(tile)
            marks.append(jnp.full((1, BLOCK), number, jnp.int32).astype(F32))
        done += total
        extra = out.shape[0] - (2 * BLOCK + STAT + 1) * total
        if extra:
            marks.append(jnp.zeros((extra, BLOCK), F32))
        out[2 * total * BLOCK :, :] = jnp.concatenate(tiles + marks, axis=0).astype(BF16)
    for copy in copies[4:]:
        copy.wait()
    for number in range(glob_ref.shape[0]):
        block = glob_ref[number]
        mine = block // blocks == me
        at = pl.ds(pl.multiple_of((block % blocks) * BLOCK, BLOCK), BLOCK)
        for turn, ref in enumerate((k_ref, v_ref)):
            first = (turn * glob_ref.shape[0] + number) * BLOCK
            rows = ref[at, :]
            own_ref[first : first + BLOCK, :] = jnp.where(mine, rows, jnp.zeros_like(rows))
    for b in range(blocks):
        rows = pl.ds(b * BLOCK, BLOCK)
        kt_ref[rows, :] = (k_ref[rows, :].astype(F32) * (1.0 / math.sqrt(width))).T.astype(BF16)


def window(heads, first, last, q_ref, g_ref, stats_ref, k_ref, v_ref, kt_ref, *rest):
    dqt_ref, dk_ref, dv_ref = rest[-3:]
    blocks = q_ref.shape[0] // BLOCK
    if first == 0:
        dk_ref[...] = jnp.zeros_like(dk_ref)
        dv_ref[...] = jnp.zeros_like(dv_ref)
    for b in range(first, last):
        rows = pl.ds(b * BLOCK, BLOCK)
        q_bd, g_bd = by_head(q_ref[rows, :], heads), by_head(g_ref[rows, :], heads)
        norm, delta = stat_rows(stats_ref[b], heads)
        total = None
        for j in range(max(b - 1, 0), min(b + 2, blocks)):
            at = pl.ds(j * BLOCK, BLOCK)
            weights_low, scores_low = weigh(k_ref[at, :], v_ref[at, :], q_bd, g_bd, norm, delta)
            term = grad_query_t(kt_ref[at, :], scores_low, heads)
            total = term if total is None else total + term
            dk_ref[at, :] += dot(scores_low, q_bd)
            dv_ref[at, :] += dot(weights_low, g_bd)
        dqt_ref[rows, :] = total


def globals_(heads, q_ref, g_ref, stats_ref, shared_ref, _, dqt_ref, part_ref, total_k, total_v):
    blocks = q_ref.shape[0] // BLOCK
    head_size = q_ref.shape[1] // heads
    rows = shared_ref.shape[0] // 2
    key_rows, value_rows = shared_ref[:rows, :], shared_ref[rows:, :]
    keys_t = (key_rows.astype(F32) * (1.0 / math.sqrt(head_size))).T.astype(BF16)
    for b in range(blocks):
        at = pl.ds(b * BLOCK, BLOCK)
        q_bd, g_bd = by_head(q_ref[at, :], heads), by_head(g_ref[at, :], heads)
        norm, delta = stat_rows(stats_ref[b], heads)
        weights_low, scores_low = weigh(key_rows, value_rows, q_bd, g_bd, norm, delta)
        dqt_ref[at, :] += grad_query_t(keys_t, scores_low, heads)
        grad_key, grad_value = dot(scores_low, q_bd), dot(weights_low, g_bd)
        if b == 0:
            total_k[...] = grad_key
            total_v[...] = grad_value
        else:
            total_k[...] += grad_key
            total_v[...] += grad_value
    part_ref[:rows, :] = total_k[...].astype(BF16)
    part_ref[rows:, :] = total_v[...].astype(BF16)


def randoms(heads, slots, refs):
    many = len(slots)
    in_refs, (k_ref, v_ref, kt_ref) = refs[:many], refs[many : many + 3]
    ret_refs, (dk_ref, dv_ref) = refs[many + 5 : 2 * many + 5], refs[2 * many + 5 :]

    def partner(in_ref, ret_ref, total):
        tail = in_ref[2 * total * BLOCK :, :].astype(F32)
        for s in range(total):
            mark = STAT * total + s
            number = jnp.max(tail[mark : mark + 1]).astype(jnp.int32)
            at = pl.ds(pl.multiple_of(number * BLOCK, BLOCK), BLOCK)
            query = in_ref[2 * s * BLOCK : (2 * s + 1) * BLOCK, :]
            grad = in_ref[(2 * s + 1) * BLOCK : (2 * s + 2) * BLOCK, :]
            q_bd, g_bd = by_head(query, heads), by_head(grad, heads)
            norm, delta = stat_rows(tail[s * STAT : (s + 1) * STAT], heads)
            weights_low, scores_low = weigh(k_ref[at, :], v_ref[at, :], q_bd, g_bd, norm, delta)
            ret_ref[s * BLOCK : (s + 1) * BLOCK, :] = grad_query_t(kt_ref[at, :], scores_low, heads).astype(BF16)
            dk_ref[at, :] += dot(scores_low, q_bd)
            dv_ref[at, :] += dot(weights_low, g_bd)

    for in_ref, ret_ref, total in zip(in_refs, ret_refs, slots):
        if len(in_ref.shape) == 2:
            partner(in_ref, ret_ref, total)
        else:
            pl.loop(0, in_ref.shape[0])(lambda n, a=in_ref, b=ret_ref, c=total: partner(a.at[n], b.at[n], c))


def finish_keys(dk_in, dv_in, total_ref, glob_ref, dk_ref, dv_ref, sum_k, sum_v):
    blocks = dk_in.shape[0] // BLOCK
    me = lax.axis_index("seq")
    many = glob_ref.shape[0]
    sum_k[...] = dk_in[...]
    sum_v[...] = dv_in[...]
    for number in range(many):
        block = glob_ref[number]

        @pl.when(block // blocks == me)
        def _():
            at = pl.ds(pl.multiple_of((block % blocks) * BLOCK, BLOCK), BLOCK)
            for turn, ref in enumerate((sum_k, sum_v)):
                first = (turn * many + number) * BLOCK
                ref[at, :] += total_ref[first : first + BLOCK, :].astype(F32)

    dk_ref[...] = sum_k[...].astype(BF16)
    dv_ref[...] = sum_v[...].astype(BF16)


def finish_queries(slots, refs):
    many = len(slots)
    dqt_ref, src_ref, ret_refs, (out_ref, total) = refs[0], refs[1], refs[2 : 2 + many], refs[-2:]
    blocks = dqt_ref.shape[0] // BLOCK
    total[...] = dqt_ref[...]
    done = 0
    for ref, many_slots in zip(ret_refs, slots):
        parts = [ref] if len(ref.shape) == 2 else [ref.at[n] for n in range(ref.shape[0])]
        for part in parts:
            for s in range(many_slots):
                b = src_ref[done]
                done += 1

                @pl.when(b >= 0)
                def _():
                    rows = pl.ds(pl.multiple_of(b * BLOCK, BLOCK), BLOCK)
                    total[rows, :] += part[s * BLOCK : (s + 1) * BLOCK, :].astype(F32)

    for b in range(blocks):
        rows = pl.ds(b * BLOCK, BLOCK)
        out_ref[rows, :] = total[rows, :].T.astype(BF16)


def shards(
    queries, keys, values, outputs, d_outputs, log_norm, rand_owner, rand_local, glob_blocks
):
    tokens, features = queries.shape
    heads = log_norm.shape[0]
    blocks = tokens // BLOCK
    many = glob_blocks.shape[0]
    owners = lax.axis_size("seq")
    references = blocks * rand_owner.shape[1]
    capacity = max(2, (references + owners - 1) // owners)
    by_permute = owners == 8
    whole = jax.ShapeDtypeStruct((tokens, features), BF16)
    wide = jax.ShapeDtypeStruct((tokens, features), F32)

    if by_permute:
        plan = [
            (capacity, (lambda me, k=k: ((me ^ k) == me + 1, (me ^ k) == me - 1)) if k in (1, 3, 7) else "xor")
            for k in range(owners)
        ]
    else:
        plan = [(capacity, None)] * owners
        plan.append((0, lambda me: (me < owners - 1, me < 0)))
        plan.append((0, lambda me: (me < 0, me > 0)))
    slots = [n + (edge not in (None, "xor")) for n, edge in plan]

    packed = call(
        lambda *refs: pack(heads, plan, refs),
        [
            whole,
            jax.ShapeDtypeStruct((blocks, STAT, BLOCK), F32),
            jax.ShapeDtypeStruct((2 * many * BLOCK, features), BF16),
            whole,
            jax.ShapeDtypeStruct((sum(slots),), jnp.int32),
        ]
        + [jax.ShapeDtypeStruct((message_rows(n), features), BF16) for n in slots],
        [VMEM] * 4 + [SMEM] + [VMEM] * len(plan),
        [HBM] * 6 + [SMEM] * 3,
        [pltpu.VMEM((tokens, features), BF16)] * 5
        + [
            pltpu.VMEM(log_norm.shape, F32),
            pltpu.SemaphoreType.DMA((6,)),
            pltpu.SMEM((owners,), jnp.int32),
            pltpu.SMEM((owners * capacity,), jnp.int32),
            pltpu.SMEM((owners * capacity,), jnp.int32),
        ],
        "pack",
        limit=LIMIT,
    )(*(pltpu.with_memory_space_constraint(x, pltpu.HBM) for x in (queries, d_outputs, outputs, keys, values, log_norm)), rand_owner.T, rand_local.T, glob_blocks)
    scaled, stats, own, keys_t, source = packed[:5]
    outgoing = packed[5:]

    def swap(array, k):
        return lax.ppermute(array, "seq", [(i, i ^ k) for i in range(owners)])

    def add_globals(shared, dqt):
        return call(
            functools.partial(globals_, heads),
            [wide, jax.ShapeDtypeStruct(own.shape, BF16)],
            [VMEM] * 2,
            [VMEM] * 5,
            [pltpu.VMEM((many * BLOCK, features), F32)] * 2,
            "globals",
            {4: 0},
        )(scaled, d_outputs, stats, shared, dqt)

    def owned(taken, counts, dk, dv):
        shapes = [
            jax.ShapeDtypeStruct(a.shape[:-2] + (n * BLOCK, features), BF16) for a, n in zip(taken, counts)
        ]
        size = len(taken)
        outs = call(
            lambda *refs: randoms(heads, counts, refs),
            shapes + [wide, wide],
            [VMEM] * (size + 2),
            [VMEM] * (size + 5),
            [],
            "randoms",
            {size + 3: size, size + 4: size + 1},
        )(*taken, keys, values, keys_t, dk, dv)
        return outs[:size], outs[size], outs[size + 1]

    def add_window(stats):
        running = ()
        cuts = [blocks * n // PIECES for n in range(PIECES + 1)]
        for first, last in zip(cuts[:-1], cuts[1:]):
            running = call(
                functools.partial(window, heads, first, last),
                [wide] * 3,
                [VMEM] * 3,
                [VMEM] * (6 + len(running)),
                [],
                "window",
                {6 + n: n for n in range(len(running))},
            )(scaled, d_outputs, stats, keys, values, keys_t, *running)
        return running

    if by_permute:
        made = {}

        def gated(name, array):
            return after(array, *[get(other) for other in GATES.get(name, ())])

        def get(name):
            if name not in made:
                made[name] = None
                made[name] = make(name)
            if made[name] is None:
                raise ValueError("cycle")
            return made[name]

        def make(name):
            kind, number = name[0], int(name[1:] or 0)
            if kind == "F":
                return swap(gated(name, outgoing[number]), number) if number else outgoing[0]
            if kind == "G":
                if number == 0:
                    return own
                base = get(f"G{number - 1}")
                return base + swap(gated(name, base), HOPS["G"][number - 1])
            if kind == "P":
                if number == 0:
                    return get("g")[1]
                base = get(f"P{number - 1}")
                other = swap(gated(name, base), HOPS["P"][number - 1])
                return (base.astype(F32) + other.astype(F32)).astype(BF16)
            if kind == "W":
                return add_window(gated(name, stats))
            if kind == "g":
                return add_globals(gated(name, get("G3")), get("W")[0])
            if kind == "R":
                before = get(f"R{number - 1}")[1:] if number else get("W")[1:]
                group = GROUPS[number]
                before = (gated(name, before[0]), before[1])
                return owned([get(f"F{k}") for k in group], [slots[k] for k in group], *before)
            if kind == "r":
                at = [n for n, group in enumerate(GROUPS) if number in group][0]
                back = get(f"R{at}")[0][GROUPS[at].index(number)]
                return swap(gated(name, back), number) if number else back

        rets = [get(f"r{k}") for k in range(owners)]
        _, dk, dv = get(f"R{len(GROUPS) - 1}")
        dqt = get("g")[0]
        part = get("P3")
        ret_slots = slots
    else:
        forward = [(i, i + 1) for i in range(owners - 1)]
        backward = [(j, i) for i, j in forward]
        everyone = lax.all_to_all(
            jnp.stack(outgoing[:owners]), "seq", split_axis=0, concat_axis=0, tiled=True
        )
        from_before = lax.ppermute(outgoing[owners], "seq", forward)
        from_after = lax.ppermute(outgoing[owners + 1], "seq", backward)
        shared = own
        step = 1
        while step < owners:
            shared = shared + swap(shared, step)
            step *= 2
        dqt, dk, dv = add_window(stats)
        dqt, part = add_globals(shared, dqt)
        step = 1
        while step < owners:
            part = (part.astype(F32) + swap(part, step).astype(F32)).astype(BF16)
            step *= 2
        backs, dk, dv = owned([everyone, from_before, from_after], [capacity, 1, 1], dk, dv)
        rets = [
            lax.all_to_all(backs[0], "seq", split_axis=0, concat_axis=0, tiled=True),
            lax.ppermute(backs[1], "seq", backward),
            lax.ppermute(backs[2], "seq", forward),
        ]
        ret_slots = [capacity, 1, 1]

    d_keys, d_values = call(
        finish_keys,
        [whole, whole],
        [VMEM] * 2,
        [VMEM] * 3 + [SMEM],
        [pltpu.VMEM((tokens, features), F32)] * 2,
        "finish_keys",
    )(dk, dv, part, glob_blocks)
    d_queries = call(
        lambda *refs: finish_queries(ret_slots, refs),
        whole,
        VMEM,
        [VMEM, SMEM] + [VMEM] * len(rets),
        [pltpu.VMEM((tokens, features), F32)],
        "finish_queries",
    )(after(dqt, d_keys), source, *rets)
    return d_queries, d_keys, d_values


def solution(mesh):
    placed = (
        P("seq", "head"),
        P("seq", "head"),
        P("seq", "head"),
        P("seq", "head"),
        P("seq", "head"),
        P("head", "seq"),
        P("seq", None),
        P("seq", None),
        P(),
    )
    return jax.shard_map(
        shards,
        mesh=mesh,
        in_specs=placed,
        out_specs=(P("seq", "head"), P("seq", "head"), P("seq", "head")),
        check_vma=False,
    )
```

```python
import functools
import math

import jax
import jax.numpy as jnp
from jax import lax
from jax.experimental import pallas as pl
from jax.experimental.pallas import tpu as pltpu
from jax.sharding import PartitionSpec as P

BLOCK = 128
STAT = 8
LOG2E = math.log2(math.e)
NT = (((1,), (1,)), ((), ()))
VMEM = pl.BlockSpec(memory_space=pltpu.VMEM)
SMEM = pl.BlockSpec(memory_space=pltpu.SMEM)
HBM = pl.BlockSpec(memory_space=pltpu.HBM)
F32 = jnp.float32
BF16 = jnp.bfloat16
LIMIT = 24
PIECES = 4
COSTS = {'window': 3, 'randoms': 3, 'finish': 3}
GATES = {'W': ['G1'], 'F5': ['G1'], 'F6': ['R0'], 'F7': ['F4'], 'F2': ['F5'], 'F3': ['F5'], 'R1': ['G2'], 'R3': ['R1'], 'r6': ['r4'], 'r7': ['r5', 'F1', 'F6'], 'P2': ['F6', 'F7', 'r4'], 'P3': ['r5', 'F5'], 'r1': ['r6'], 'R0': ['G2']}
GROUPS = [[4], [0], [5], [1], [2], [6], [7], [3]]
HOPS = {'G': [4, 2, 1], 'P': [1, 2, 4]}


def call(body, out_shape, out_specs, in_specs, scratch, name, aliases={}, limit=24):
    return pl.pallas_call(
        body,
        out_shape=out_shape,
        in_specs=in_specs,
        out_specs=out_specs,
        scratch_shapes=scratch,
        input_output_aliases=aliases,
        compiler_params=pltpu.CompilerParams(vmem_limit_bytes=int(limit * 1024 * 1024)),
        cost_estimate=pl.CostEstimate(
            flops=int(COSTS.get(name, 0) * 1.15e9), bytes_accessed=0, transcendentals=0
        ),
        name=name,
    )


def after(array, *others):
    return lax.optimization_barrier((array, *others))[0] if others else array


def dot(a, b):
    return jnp.dot(a, b, preferred_element_type=F32)


def by_head(rows, heads):
    width = rows.shape[1] // heads
    lane = lax.broadcasted_iota(jnp.int32, (1, rows.shape[1]), 1)
    parts = []
    for h in range(heads):
        keep = ((lane >= h * width) & (lane < (h + 1) * width)).astype(F32).astype(BF16)
        parts.append(rows * keep)
    return jnp.concatenate(parts, axis=0)


def stat_rows(tile, heads):
    half = 2 * heads
    norm = [tile[h : h + 1] + tile[heads + h : heads + h + 1] for h in range(heads)]
    delta = [tile[half + h : half + h + 1] + tile[half + heads + h : half + heads + h + 1] for h in range(heads)]
    return jnp.concatenate(norm, axis=1), jnp.concatenate(delta, axis=1)


def weigh(key_rows, value_rows, q_bd, g_bd, norm, delta):
    scores = lax.dot_general(key_rows, q_bd, NT, preferred_element_type=F32)
    weights = jnp.exp2(scores * LOG2E - norm)
    grad = lax.dot_general(value_rows, g_bd, NT, preferred_element_type=F32)
    return weights.astype(BF16), (weights * (grad - delta)).astype(BF16)


def grad_query_t(keys_t, low, heads):
    width = keys_t.shape[0] // heads
    return jnp.concatenate(
        [dot(keys_t[h * width : (h + 1) * width], low[:, h * BLOCK : (h + 1) * BLOCK]) for h in range(heads)],
        axis=0,
    )


def message_rows(slots):
    return -(-((2 * BLOCK + STAT + 1) * slots) // 16) * 16


def pick_globals(blocks, k_hbm, v_hbm, glob_ref, own_ref, sems):
    many = glob_ref.shape[0]
    me = lax.axis_index("seq")
    own_ref[...] = jnp.zeros_like(own_ref)
    for waiting in (False, True):
        for number in range(many):
            block = glob_ref[number]

            @pl.when(block // blocks == me)
            def _():
                at = pl.ds(pl.multiple_of((block % blocks) * BLOCK, BLOCK), BLOCK)
                for turn, ref in enumerate((k_hbm, v_hbm)):
                    place = turn * many + number
                    copy = pltpu.make_async_copy(
                        ref.at[at, :], own_ref.at[pl.ds(place * BLOCK, BLOCK), :], sems.at[place]
                    )
                    copy.wait() if waiting else copy.start()


def pack(heads, plan, refs):
    q_hbm, g_hbm, o_hbm, k_hbm, norm_hbm, owner_hbm, local_hbm = refs[:7]
    scaled_ref, stats_ref, kt_ref, src_ref = refs[7:11]
    out_refs = refs[11 : 11 + len(plan)]
    q_ref, g_ref, o_ref, k_ref, norm_ref, owner_ref, local_ref, sems, count, source, place = refs[11 + len(plan) :]
    copies = [
        pltpu.make_async_copy(a, b, sems.at[n])
        for n, (a, b) in enumerate(
            (
                (owner_hbm, owner_ref),
                (local_hbm, local_ref),
                (g_hbm, g_ref),
                (o_hbm, o_ref),
                (norm_hbm, norm_ref),
                (q_hbm, q_ref),
                (k_hbm, k_ref),
            )
        )
    ]
    for copy in copies:
        copy.start()
    blocks = q_ref.shape[0] // BLOCK
    per_block = owner_ref.shape[0]
    width = q_ref.shape[1] // heads
    me = lax.axis_index("seq")
    fold = any(entry[1] == "xor" for entry in plan)
    most = max(entry[0] for entry in plan)
    randoms = sum(1 for entry in plan if entry[0])
    for copy in copies[:2]:
        copy.wait()
    for k in range(randoms):
        count[k] = 0
        for s in range(most):
            source[k * most + s] = -1
    for b in range(blocks):
        for r in range(per_block):
            k = owner_ref[r, b]
            if fold:
                k = k ^ me
            s = count[k]
            count[k] = s + 1
            source[k * most + s] = b
            place[k * most + s] = local_ref[r, b]
    for copy in copies[2:5]:
        copy.wait()
    for b in range(blocks):
        rows = pl.ds(b * BLOCK, BLOCK)
        prod = (o_ref[rows, :].astype(F32) * g_ref[rows, :].astype(F32)).T
        norm = [norm_ref[h : h + 1, rows] * LOG2E for h in range(heads)]
        delta = [jnp.sum(prod[h * width : (h + 1) * width], axis=0, keepdims=True) for h in range(heads)]
        exact = jnp.concatenate(norm + delta, axis=0)
        high = exact.astype(BF16).astype(F32)
        low = (exact - high).astype(BF16).astype(F32)
        stats_ref[b] = jnp.concatenate([high[:heads], low[:heads], high[heads:], low[heads:]], axis=0)
    copies[5].wait()
    scaled_ref[...] = q_ref[...] * jnp.asarray(1.0 / math.sqrt(width), BF16)
    full = blocks * per_block == randoms * most
    done = 0
    for k, (slots, edge) in enumerate(plan):
        out = out_refs[k]
        tiles, marks = [], []
        total = slots + (edge not in (None, "xor"))
        for s in range(total):
            if s < slots:
                b, number, sure = source[k * most + s], place[k * most + s], full
            else:
                up, down = edge(me)
                b = jnp.where(up, blocks - 1, jnp.where(down, 0, -1))
                number, sure = jnp.where(up, 0, blocks - 1), False
            src_ref[done + s] = b
            safe = jnp.maximum(b, 0)
            at = pl.ds(pl.multiple_of(safe * BLOCK, BLOCK), BLOCK)
            query, grad, tile = scaled_ref[at, :], g_ref[at, :], stats_ref[safe]
            if not sure:
                query = jnp.where(b >= 0, query, jnp.zeros_like(query))
                grad = jnp.where(b >= 0, grad, jnp.zeros_like(grad))
                tile = jnp.where(b >= 0, tile, jnp.zeros_like(tile))
                number = jnp.where(b >= 0, number, 0)
            out[2 * s * BLOCK : (2 * s + 1) * BLOCK, :] = query
            out[(2 * s + 1) * BLOCK : (2 * s + 2) * BLOCK, :] = grad
            tiles.append(tile)
            marks.append(jnp.full((1, BLOCK), number, jnp.int32).astype(F32))
        done += total
        extra = out.shape[0] - (2 * BLOCK + STAT + 1) * total
        if extra:
            marks.append(jnp.zeros((extra, BLOCK), F32))
        out[2 * total * BLOCK :, :] = jnp.concatenate(tiles + marks, axis=0).astype(BF16)
    copies[6].wait()
    for b in range(blocks):
        rows = pl.ds(b * BLOCK, BLOCK)
        kt_ref[rows, :] = (k_ref[rows, :].astype(F32) * (1.0 / math.sqrt(width))).T.astype(BF16)


def window(heads, first, last, q_ref, g_ref, stats_ref, k_ref, v_ref, kt_ref, *rest):
    dqt_ref, dk_ref, dv_ref = rest[-3:]
    blocks = q_ref.shape[0] // BLOCK
    if first == 0:
        dk_ref[...] = jnp.zeros_like(dk_ref)
        dv_ref[...] = jnp.zeros_like(dv_ref)
    for b in range(first, last):
        rows = pl.ds(b * BLOCK, BLOCK)
        q_bd, g_bd = by_head(q_ref[rows, :], heads), by_head(g_ref[rows, :], heads)
        norm, delta = stat_rows(stats_ref[b], heads)
        total = None
        for j in range(max(b - 1, 0), min(b + 2, blocks)):
            at = pl.ds(j * BLOCK, BLOCK)
            weights_low, scores_low = weigh(k_ref[at, :], v_ref[at, :], q_bd, g_bd, norm, delta)
            term = grad_query_t(kt_ref[at, :], scores_low, heads)
            total = term if total is None else total + term
            dk_ref[at, :] += dot(scores_low, q_bd)
            dv_ref[at, :] += dot(weights_low, g_bd)
        dqt_ref[rows, :] = total


def globals_(heads, q_ref, g_ref, stats_ref, shared_ref, _, dqt_ref, part_ref, total_k, total_v):
    blocks = q_ref.shape[0] // BLOCK
    head_size = q_ref.shape[1] // heads
    rows = shared_ref.shape[0] // 2
    key_rows, value_rows = shared_ref[:rows, :], shared_ref[rows:, :]
    keys_t = (key_rows.astype(F32) * (1.0 / math.sqrt(head_size))).T.astype(BF16)
    for b in range(blocks):
        at = pl.ds(b * BLOCK, BLOCK)
        q_bd, g_bd = by_head(q_ref[at, :], heads), by_head(g_ref[at, :], heads)
        norm, delta = stat_rows(stats_ref[b], heads)
        weights_low, scores_low = weigh(key_rows, value_rows, q_bd, g_bd, norm, delta)
        dqt_ref[at, :] += grad_query_t(keys_t, scores_low, heads)
        grad_key, grad_value = dot(scores_low, q_bd), dot(weights_low, g_bd)
        if b == 0:
            total_k[...] = grad_key
            total_v[...] = grad_value
        else:
            total_k[...] += grad_key
            total_v[...] += grad_value
    part_ref[:rows, :] = total_k[...].astype(BF16)
    part_ref[rows:, :] = total_v[...].astype(BF16)


def randoms(heads, slots, refs):
    many = len(slots)
    in_refs, (k_ref, v_ref, kt_ref) = refs[:many], refs[many : many + 3]
    ret_refs, (dk_ref, dv_ref) = refs[many + 5 : 2 * many + 5], refs[2 * many + 5 :]

    def partner(in_ref, ret_ref, total):
        tail = in_ref[2 * total * BLOCK :, :].astype(F32)
        for s in range(total):
            mark = STAT * total + s
            number = jnp.max(tail[mark : mark + 1]).astype(jnp.int32)
            at = pl.ds(pl.multiple_of(number * BLOCK, BLOCK), BLOCK)
            query = in_ref[2 * s * BLOCK : (2 * s + 1) * BLOCK, :]
            grad = in_ref[(2 * s + 1) * BLOCK : (2 * s + 2) * BLOCK, :]
            q_bd, g_bd = by_head(query, heads), by_head(grad, heads)
            norm, delta = stat_rows(tail[s * STAT : (s + 1) * STAT], heads)
            weights_low, scores_low = weigh(k_ref[at, :], v_ref[at, :], q_bd, g_bd, norm, delta)
            ret_ref[s * BLOCK : (s + 1) * BLOCK, :] = grad_query_t(kt_ref[at, :], scores_low, heads).astype(BF16)
            dk_ref[at, :] += dot(scores_low, q_bd)
            dv_ref[at, :] += dot(weights_low, g_bd)

    for in_ref, ret_ref, total in zip(in_refs, ret_refs, slots):
        if len(in_ref.shape) == 2:
            partner(in_ref, ret_ref, total)
        else:
            pl.loop(0, in_ref.shape[0])(lambda n, a=in_ref, b=ret_ref, c=total: partner(a.at[n], b.at[n], c))


def finish(slots, refs):
    dqt_ref, dk_in, dv_in, total_ref, glob_hbm, src_hbm = refs[:6]
    ret_refs = refs[6 : 6 + len(slots)]
    q_hbm, k_hbm, v_hbm, sum_q, sum_k, sum_v, q_out, k_out, v_out, glob_ref, src_ref, sems = refs[6 + len(slots) :]
    blocks = dk_in.shape[0] // BLOCK
    many = glob_ref.shape[0]
    me = lax.axis_index("seq")
    names = [
        pltpu.make_async_copy(a, b, sems.at[n]) for n, (a, b) in enumerate(((glob_hbm, glob_ref), (src_hbm, src_ref)))
    ]
    for copy in names:
        copy.start()
    sum_k[...] = dk_in[...]
    sum_v[...] = dv_in[...]
    sum_q[...] = dqt_ref[...]
    for copy in names:
        copy.wait()
    for number in range(many):
        block = glob_ref[number]

        @pl.when(block // blocks == me)
        def _():
            at = pl.ds(pl.multiple_of((block % blocks) * BLOCK, BLOCK), BLOCK)
            for turn, ref in enumerate((sum_k, sum_v)):
                first = (turn * many + number) * BLOCK
                ref[at, :] += total_ref[first : first + BLOCK, :].astype(F32)

    k_out[...] = sum_k[...].astype(BF16)
    v_out[...] = sum_v[...].astype(BF16)
    copies = [
        pltpu.make_async_copy(a, b, sems.at[2 + n])
        for n, (a, b) in enumerate(((k_out, k_hbm), (v_out, v_hbm), (q_out, q_hbm)))
    ]
    copies[0].start()
    copies[1].start()
    done = 0
    for ref, many_slots in zip(ret_refs, slots):
        parts = [ref] if len(ref.shape) == 2 else [ref.at[n] for n in range(ref.shape[0])]
        for part in parts:
            for s in range(many_slots):
                b = src_ref[done]
                done += 1

                @pl.when(b >= 0)
                def _():
                    rows = pl.ds(pl.multiple_of(b * BLOCK, BLOCK), BLOCK)
                    sum_q[rows, :] += part[s * BLOCK : (s + 1) * BLOCK, :].astype(F32)

    for b in range(blocks):
        rows = pl.ds(b * BLOCK, BLOCK)
        q_out[rows, :] = sum_q[rows, :].T.astype(BF16)
    copies[2].start()
    for copy in copies:
        copy.wait()


def shards(
    queries, keys, values, outputs, d_outputs, log_norm, rand_owner, rand_local, glob_blocks
):
    tokens, features = queries.shape
    heads = log_norm.shape[0]
    blocks = tokens // BLOCK
    many = glob_blocks.shape[0]
    owners = lax.axis_size("seq")
    references = blocks * rand_owner.shape[1]
    capacity = max(2, (references + owners - 1) // owners)
    by_permute = owners == 8
    whole = jax.ShapeDtypeStruct((tokens, features), BF16)
    wide = jax.ShapeDtypeStruct((tokens, features), F32)

    if by_permute:
        plan = [
            (capacity, (lambda me, k=k: ((me ^ k) == me + 1, (me ^ k) == me - 1)) if k in (1, 3, 7) else "xor")
            for k in range(owners)
        ]
    else:
        plan = [(capacity, None)] * owners
        plan.append((0, lambda me: (me < owners - 1, me < 0)))
        plan.append((0, lambda me: (me < 0, me > 0)))
    slots = [n + (edge not in (None, "xor")) for n, edge in plan]

    def in_hbm(*arrays):
        return [pltpu.with_memory_space_constraint(array, pltpu.HBM) for array in arrays]

    own = call(
        functools.partial(pick_globals, blocks),
        jax.ShapeDtypeStruct((2 * many * BLOCK, features), BF16),
        VMEM,
        [HBM] * 2 + [SMEM],
        [pltpu.SemaphoreType.DMA((2 * many,))],
        "pick_globals",
    )(*in_hbm(keys, values), glob_blocks)
    packed = call(
        lambda *refs: pack(heads, plan, refs),
        [
            whole,
            jax.ShapeDtypeStruct((blocks, STAT, BLOCK), F32),
            whole,
            jax.ShapeDtypeStruct((sum(slots),), jnp.int32),
        ]
        + [jax.ShapeDtypeStruct((message_rows(n), features), BF16) for n in slots],
        [VMEM] * 3 + [SMEM] + [VMEM] * len(plan),
        [HBM] * 7,
        [pltpu.VMEM((tokens, features), BF16)] * 4
        + [
            pltpu.VMEM(log_norm.shape, F32),
            pltpu.SMEM(rand_owner.shape[::-1], jnp.int32),
            pltpu.SMEM(rand_local.shape[::-1], jnp.int32),
            pltpu.SemaphoreType.DMA((7,)),
            pltpu.SMEM((owners,), jnp.int32),
            pltpu.SMEM((owners * capacity,), jnp.int32),
            pltpu.SMEM((owners * capacity,), jnp.int32),
        ],
        "pack",
    )(*in_hbm(queries, d_outputs, outputs, keys, log_norm, rand_owner.T, rand_local.T))
    scaled, stats, keys_t, source = packed[:4]
    outgoing = packed[4:]

    def swap(array, k):
        return lax.ppermute(array, "seq", [(i, i ^ k) for i in range(owners)])

    def add_globals(shared, dqt):
        return call(
            functools.partial(globals_, heads),
            [wide, jax.ShapeDtypeStruct(own.shape, BF16)],
            [VMEM] * 2,
            [VMEM] * 5,
            [pltpu.VMEM((many * BLOCK, features), F32)] * 2,
            "globals",
            {4: 0},
        )(scaled, d_outputs, stats, shared, dqt)

    def owned(taken, counts, dk, dv):
        shapes = [
            jax.ShapeDtypeStruct(a.shape[:-2] + (n * BLOCK, features), BF16) for a, n in zip(taken, counts)
        ]
        size = len(taken)
        outs = call(
            lambda *refs: randoms(heads, counts, refs),
            shapes + [wide, wide],
            [VMEM] * (size + 2),
            [VMEM] * (size + 5),
            [],
            "randoms",
            {size + 3: size, size + 4: size + 1},
        )(*taken, keys, values, keys_t, dk, dv)
        return outs[:size], outs[size], outs[size + 1]

    def add_window(stats):
        running = ()
        cuts = [blocks * n // PIECES for n in range(PIECES + 1)]
        for first, last in zip(cuts[:-1], cuts[1:]):
            running = call(
                functools.partial(window, heads, first, last),
                [wide] * 3,
                [VMEM] * 3,
                [VMEM] * (6 + len(running)),
                [],
                "window",
                {6 + n: n for n in range(len(running))},
            )(scaled, d_outputs, stats, keys, values, keys_t, *running)
        return running

    if by_permute:
        made = {}

        def gated(name, array):
            others = [get(other) for other in GATES.get(name, ())]
            return after(array, *[x if isinstance(x, jax.Array) else x[0] for x in others])

        def get(name):
            if name not in made:
                made[name] = None
                made[name] = make(name)
            if made[name] is None:
                raise ValueError("cycle")
            return made[name]

        def make(name):
            kind, number = name[0], int(name[1:] or 0)
            if kind == "F":
                return swap(gated(name, outgoing[number]), number) if number else outgoing[0]
            if kind == "G":
                if number == 0:
                    return own
                base = get(f"G{number - 1}")
                return base + swap(gated(name, base), HOPS["G"][number - 1])
            if kind == "P":
                if number == 0:
                    return get("g")[0]
                base = get(f"P{number - 1}")
                other = swap(gated(name, base), HOPS["P"][number - 1])
                return (base.astype(F32) + other.astype(F32)).astype(BF16)
            if kind == "W":
                return add_window(gated(name, stats))
            if kind == "g":
                return add_globals(gated(name, get("G3")), get("W")[0])[::-1]
            if kind == "R":
                before = get(f"R{number - 1}")[1:] if number else get("W")[1:]
                group = GROUPS[number]
                before = (gated(name, before[0]), before[1])
                return owned([get(f"F{k}") for k in group], [slots[k] for k in group], *before)
            if kind == "r":
                at = [n for n, group in enumerate(GROUPS) if number in group][0]
                back = get(f"R{at}")[0][GROUPS[at].index(number)]
                return swap(gated(name, back), number) if number else back

        rets = [get(f"r{k}") for k in range(owners)]
        _, dk, dv = get(f"R{len(GROUPS) - 1}")
        dqt = get("g")[1]
        part = get("P3")
        ret_slots = slots
    else:
        forward = [(i, i + 1) for i in range(owners - 1)]
        backward = [(j, i) for i, j in forward]
        everyone = lax.all_to_all(
            jnp.stack(outgoing[:owners]), "seq", split_axis=0, concat_axis=0, tiled=True
        )
        from_before = lax.ppermute(outgoing[owners], "seq", forward)
        from_after = lax.ppermute(outgoing[owners + 1], "seq", backward)
        shared = own
        step = 1
        while step < owners:
            shared = shared + swap(shared, step)
            step *= 2
        dqt, dk, dv = add_window(stats)
        dqt, part = add_globals(shared, dqt)
        step = 1
        while step < owners:
            part = (part.astype(F32) + swap(part, step).astype(F32)).astype(BF16)
            step *= 2
        backs, dk, dv = owned([everyone, from_before, from_after], [capacity, 1, 1], dk, dv)
        rets = [
            lax.all_to_all(backs[0], "seq", split_axis=0, concat_axis=0, tiled=True),
            lax.ppermute(backs[1], "seq", backward),
            lax.ppermute(backs[2], "seq", forward),
        ]
        ret_slots = [capacity, 1, 1]

    return call(
        lambda *refs: finish(ret_slots, refs),
        [whole] * 3,
        [HBM] * 3,
        [VMEM] * 4 + [HBM] * 2 + [VMEM] * len(rets),
        [pltpu.VMEM((tokens, features), F32)] * 3
        + [pltpu.VMEM((tokens, features), BF16)] * 3
        + [
            pltpu.SMEM(glob_blocks.shape, jnp.int32),
            pltpu.SMEM(source.shape, jnp.int32),
            pltpu.SemaphoreType.DMA((5,)),
        ],
        "finish",
    )(dqt, dk, dv, part, *in_hbm(glob_blocks, source), *rets)


def solution(mesh):
    placed = (
        P("seq", "head"),
        P("seq", "head"),
        P("seq", "head"),
        P("seq", "head"),
        P("seq", "head"),
        P("head", "seq"),
        P("seq", None),
        P("seq", None),
        P(),
    )
    return jax.shard_map(
        shards,
        mesh=mesh,
        in_specs=placed,
        out_specs=(P("seq", "head"), P("seq", "head"), P("seq", "head")),
        check_vma=False,
    )
```

```python
import functools
import math

import jax
import jax.numpy as jnp
from jax import lax
from jax.experimental import pallas as pl
from jax.experimental.pallas import tpu as pltpu
from jax.sharding import PartitionSpec as P

BLOCK = 128
STAT = 8
LOG2E = math.log2(math.e)
NT = (((1,), (1,)), ((), ()))
VMEM = pl.BlockSpec(memory_space=pltpu.VMEM)
SMEM = pl.BlockSpec(memory_space=pltpu.SMEM)
HBM = pl.BlockSpec(memory_space=pltpu.HBM)
F32 = jnp.float32
BF16 = jnp.bfloat16
LIMIT = 24
PIECES = 2
COSTS = {'window': 3, 'randoms': 3, 'finish': 3}
GATES = {'W': ['G1'], 'F5': ['G1'], 'F6': ['R0'], 'F7': ['F4'], 'F2': ['F5'], 'F3': ['F5'], 'R1': ['G2'], 'r6': ['r4'], 'r7': ['r5', 'F1', 'F6'], 'P2': ['F6', 'F7', 'r4'], 'P3': ['r5', 'F5'], 'r1': ['r6'], 'R0': ['G2'], 'G3': ['R1']}
GROUPS = [[4], [0], [5], [1], [2, 6], [7], [3]]
HOPS = {'G': [4, 2, 1], 'P': [1, 2, 4]}


def call(body, out_shape, out_specs, in_specs, scratch, name, aliases={}, limit=24):
    return pl.pallas_call(
        body,
        out_shape=out_shape,
        in_specs=in_specs,
        out_specs=out_specs,
        scratch_shapes=scratch,
        input_output_aliases=aliases,
        compiler_params=pltpu.CompilerParams(vmem_limit_bytes=int(limit * 1024 * 1024)),
        cost_estimate=pl.CostEstimate(
            flops=int(COSTS.get(name, 0) * 1.15e9), bytes_accessed=0, transcendentals=0
        ),
        name=name,
    )


def after(array, *others):
    return lax.optimization_barrier((array, *others))[0] if others else array


def dot(a, b):
    return jnp.dot(a, b, preferred_element_type=F32)


def by_head(rows, heads):
    width = rows.shape[1] // heads
    lane = lax.broadcasted_iota(jnp.int32, (1, rows.shape[1]), 1)
    parts = []
    for h in range(heads):
        keep = ((lane >= h * width) & (lane < (h + 1) * width)).astype(F32).astype(BF16)
        parts.append(rows * keep)
    return jnp.concatenate(parts, axis=0)


def stat_rows(tile, heads):
    half = 2 * heads
    norm = [tile[h : h + 1] + tile[heads + h : heads + h + 1] for h in range(heads)]
    delta = [tile[half + h : half + h + 1] + tile[half + heads + h : half + heads + h + 1] for h in range(heads)]
    return jnp.concatenate(norm, axis=1), jnp.concatenate(delta, axis=1)


def weigh(key_rows, value_rows, q_bd, g_bd, norm, delta):
    scores = lax.dot_general(key_rows, q_bd, NT, preferred_element_type=F32)
    weights = jnp.exp2(scores * LOG2E - norm)
    grad = lax.dot_general(value_rows, g_bd, NT, preferred_element_type=F32)
    return weights.astype(BF16), (weights * (grad - delta)).astype(BF16)


def grad_query_t(keys_t, low, heads):
    width = keys_t.shape[0] // heads
    return jnp.concatenate(
        [dot(keys_t[h * width : (h + 1) * width], low[:, h * BLOCK : (h + 1) * BLOCK]) for h in range(heads)],
        axis=0,
    )


def message_rows(slots):
    return -(-((2 * BLOCK + STAT + 1) * slots) // 16) * 16


def pick_globals(blocks, k_hbm, v_hbm, glob_ref, own_ref, sems):
    many = glob_ref.shape[0]
    me = lax.axis_index("seq")
    own_ref[...] = jnp.zeros_like(own_ref)
    for waiting in (False, True):
        for number in range(many):
            block = glob_ref[number]

            @pl.when(block // blocks == me)
            def _():
                at = pl.ds(pl.multiple_of((block % blocks) * BLOCK, BLOCK), BLOCK)
                for turn, ref in enumerate((k_hbm, v_hbm)):
                    place = turn * many + number
                    copy = pltpu.make_async_copy(
                        ref.at[at, :], own_ref.at[pl.ds(place * BLOCK, BLOCK), :], sems.at[place]
                    )
                    copy.wait() if waiting else copy.start()


def pack(heads, plan, refs):
    q_hbm, g_hbm, o_hbm, k_hbm, norm_hbm, owner_hbm, local_hbm = refs[:7]
    scaled_ref, stats_ref, kt_ref, src_ref = refs[7:11]
    out_refs = refs[11 : 11 + len(plan)]
    q_ref, g_ref, o_ref, k_ref, norm_ref, owner_ref, local_ref, sems, count, source, place = refs[11 + len(plan) :]
    copies = [
        pltpu.make_async_copy(a, b, sems.at[n])
        for n, (a, b) in enumerate(
            (
                (owner_hbm, owner_ref),
                (local_hbm, local_ref),
                (g_hbm, g_ref),
                (o_hbm, o_ref),
                (norm_hbm, norm_ref),
                (q_hbm, q_ref),
                (k_hbm, k_ref),
            )
        )
    ]
    for copy in copies:
        copy.start()
    blocks = q_ref.shape[0] // BLOCK
    per_block = owner_ref.shape[0]
    width = q_ref.shape[1] // heads
    me = lax.axis_index("seq")
    fold = any(entry[1] == "xor" for entry in plan)
    most = max(entry[0] for entry in plan)
    randoms = sum(1 for entry in plan if entry[0])
    for copy in copies[:2]:
        copy.wait()
    for k in range(randoms):
        count[k] = 0
        for s in range(most):
            source[k * most + s] = -1
    for b in range(blocks):
        for r in range(per_block):
            k = owner_ref[r, b]
            if fold:
                k = k ^ me
            s = count[k]
            count[k] = s + 1
            source[k * most + s] = b
            place[k * most + s] = local_ref[r, b]
    for copy in copies[2:5]:
        copy.wait()
    for b in range(blocks):
        rows = pl.ds(b * BLOCK, BLOCK)
        prod = (o_ref[rows, :].astype(F32) * g_ref[rows, :].astype(F32)).T
        norm = [norm_ref[h : h + 1, rows] * LOG2E for h in range(heads)]
        delta = [jnp.sum(prod[h * width : (h + 1) * width], axis=0, keepdims=True) for h in range(heads)]
        exact = jnp.concatenate(norm + delta, axis=0)
        high = exact.astype(BF16).astype(F32)
        low = (exact - high).astype(BF16).astype(F32)
        stats_ref[b] = jnp.concatenate([high[:heads], low[:heads], high[heads:], low[heads:]], axis=0)
    copies[5].wait()
    scaled_ref[...] = q_ref[...] * jnp.asarray(1.0 / math.sqrt(width), BF16)
    full = blocks * per_block == randoms * most
    done = 0
    for k, (slots, edge) in enumerate(plan):
        out = out_refs[k]
        tiles, marks = [], []
        total = slots + (edge not in (None, "xor"))
        for s in range(total):
            if s < slots:
                b, number, sure = source[k * most + s], place[k * most + s], full
            else:
                up, down = edge(me)
                b = jnp.where(up, blocks - 1, jnp.where(down, 0, -1))
                number, sure = jnp.where(up, 0, blocks - 1), False
            src_ref[done + s] = b
            safe = jnp.maximum(b, 0)
            at = pl.ds(pl.multiple_of(safe * BLOCK, BLOCK), BLOCK)
            query, grad, tile = scaled_ref[at, :], g_ref[at, :], stats_ref[safe]
            if not sure:
                query = jnp.where(b >= 0, query, jnp.zeros_like(query))
                grad = jnp.where(b >= 0, grad, jnp.zeros_like(grad))
                tile = jnp.where(b >= 0, tile, jnp.zeros_like(tile))
                number = jnp.where(b >= 0, number, 0)
            out[2 * s * BLOCK : (2 * s + 1) * BLOCK, :] = query
            out[(2 * s + 1) * BLOCK : (2 * s + 2) * BLOCK, :] = grad
            tiles.append(tile)
            marks.append(jnp.full((1, BLOCK), number, jnp.int32).astype(F32))
        done += total
        extra = out.shape[0] - (2 * BLOCK + STAT + 1) * total
        if extra:
            marks.append(jnp.zeros((extra, BLOCK), F32))
        out[2 * total * BLOCK :, :] = jnp.concatenate(tiles + marks, axis=0).astype(BF16)
    copies[6].wait()
    for b in range(blocks):
        rows = pl.ds(b * BLOCK, BLOCK)
        kt_ref[rows, :] = (k_ref[rows, :].astype(F32) * (1.0 / math.sqrt(width))).T.astype(BF16)


def window(heads, first, last, q_ref, g_ref, stats_ref, k_ref, v_ref, kt_ref, *rest):
    dqt_ref, dk_ref, dv_ref = rest[-3:]
    blocks = q_ref.shape[0] // BLOCK
    if first == 0:
        dk_ref[...] = jnp.zeros_like(dk_ref)
        dv_ref[...] = jnp.zeros_like(dv_ref)
    for b in range(first, last):
        rows = pl.ds(b * BLOCK, BLOCK)
        q_bd, g_bd = by_head(q_ref[rows, :], heads), by_head(g_ref[rows, :], heads)
        norm, delta = stat_rows(stats_ref[b], heads)
        total = None
        for j in range(max(b - 1, 0), min(b + 2, blocks)):
            at = pl.ds(j * BLOCK, BLOCK)
            weights_low, scores_low = weigh(k_ref[at, :], v_ref[at, :], q_bd, g_bd, norm, delta)
            term = grad_query_t(kt_ref[at, :], scores_low, heads)
            total = term if total is None else total + term
            dk_ref[at, :] += dot(scores_low, q_bd)
            dv_ref[at, :] += dot(weights_low, g_bd)
        dqt_ref[rows, :] = total


def globals_(heads, q_ref, g_ref, stats_ref, shared_ref, _, dqt_ref, part_ref, total_k, total_v):
    blocks = q_ref.shape[0] // BLOCK
    head_size = q_ref.shape[1] // heads
    rows = shared_ref.shape[0] // 2
    key_rows, value_rows = shared_ref[:rows, :], shared_ref[rows:, :]
    keys_t = (key_rows.astype(F32) * (1.0 / math.sqrt(head_size))).T.astype(BF16)
    for b in range(blocks):
        at = pl.ds(b * BLOCK, BLOCK)
        q_bd, g_bd = by_head(q_ref[at, :], heads), by_head(g_ref[at, :], heads)
        norm, delta = stat_rows(stats_ref[b], heads)
        weights_low, scores_low = weigh(key_rows, value_rows, q_bd, g_bd, norm, delta)
        dqt_ref[at, :] += grad_query_t(keys_t, scores_low, heads)
        grad_key, grad_value = dot(scores_low, q_bd), dot(weights_low, g_bd)
        if b == 0:
            total_k[...] = grad_key
            total_v[...] = grad_value
        else:
            total_k[...] += grad_key
            total_v[...] += grad_value
    part_ref[:rows, :] = total_k[...].astype(BF16)
    part_ref[rows:, :] = total_v[...].astype(BF16)


def randoms(heads, slots, refs):
    many = len(slots)
    in_refs, (k_ref, v_ref, kt_ref) = refs[:many], refs[many : many + 3]
    ret_refs, (dk_ref, dv_ref) = refs[many + 5 : 2 * many + 5], refs[2 * many + 5 :]

    def partner(in_ref, ret_ref, total):
        tail = in_ref[2 * total * BLOCK :, :].astype(F32)
        for s in range(total):
            mark = STAT * total + s
            number = jnp.max(tail[mark : mark + 1]).astype(jnp.int32)
            at = pl.ds(pl.multiple_of(number * BLOCK, BLOCK), BLOCK)
            query = in_ref[2 * s * BLOCK : (2 * s + 1) * BLOCK, :]
            grad = in_ref[(2 * s + 1) * BLOCK : (2 * s + 2) * BLOCK, :]
            q_bd, g_bd = by_head(query, heads), by_head(grad, heads)
            norm, delta = stat_rows(tail[s * STAT : (s + 1) * STAT], heads)
            weights_low, scores_low = weigh(k_ref[at, :], v_ref[at, :], q_bd, g_bd, norm, delta)
            ret_ref[s * BLOCK : (s + 1) * BLOCK, :] = grad_query_t(kt_ref[at, :], scores_low, heads).astype(BF16)
            dk_ref[at, :] += dot(scores_low, q_bd)
            dv_ref[at, :] += dot(weights_low, g_bd)

    for in_ref, ret_ref, total in zip(in_refs, ret_refs, slots):
        if len(in_ref.shape) == 2:
            partner(in_ref, ret_ref, total)
        else:
            pl.loop(0, in_ref.shape[0])(lambda n, a=in_ref, b=ret_ref, c=total: partner(a.at[n], b.at[n], c))


def finish(slots, refs):
    dqt_ref, dk_in, dv_in, total_ref, glob_hbm, src_hbm = refs[:6]
    ret_refs = refs[6 : 6 + len(slots)]
    q_hbm, k_hbm, v_hbm, sum_q, sum_k, sum_v, q_out, k_out, v_out, glob_ref, src_ref, sems = refs[6 + len(slots) :]
    blocks = dk_in.shape[0] // BLOCK
    many = glob_ref.shape[0]
    me = lax.axis_index("seq")
    names = [
        pltpu.make_async_copy(a, b, sems.at[n]) for n, (a, b) in enumerate(((glob_hbm, glob_ref), (src_hbm, src_ref)))
    ]
    for copy in names:
        copy.start()
    sum_k[...] = dk_in[...]
    sum_v[...] = dv_in[...]
    sum_q[...] = dqt_ref[...]
    for copy in names:
        copy.wait()
    for number in range(many):
        block = glob_ref[number]

        @pl.when(block // blocks == me)
        def _():
            at = pl.ds(pl.multiple_of((block % blocks) * BLOCK, BLOCK), BLOCK)
            for turn, ref in enumerate((sum_k, sum_v)):
                first = (turn * many + number) * BLOCK
                ref[at, :] += total_ref[first : first + BLOCK, :].astype(F32)

    k_out[...] = sum_k[...].astype(BF16)
    v_out[...] = sum_v[...].astype(BF16)
    copies = [
        pltpu.make_async_copy(a, b, sems.at[2 + n])
        for n, (a, b) in enumerate(((k_out, k_hbm), (v_out, v_hbm), (q_out, q_hbm)))
    ]
    copies[0].start()
    copies[1].start()
    done = 0
    for ref, many_slots in zip(ret_refs, slots):
        parts = [ref] if len(ref.shape) == 2 else [ref.at[n] for n in range(ref.shape[0])]
        for part in parts:
            for s in range(many_slots):
                b = src_ref[done]
                done += 1

                @pl.when(b >= 0)
                def _():
                    rows = pl.ds(pl.multiple_of(b * BLOCK, BLOCK), BLOCK)
                    sum_q[rows, :] += part[s * BLOCK : (s + 1) * BLOCK, :].astype(F32)

    for b in range(blocks):
        rows = pl.ds(b * BLOCK, BLOCK)
        q_out[rows, :] = sum_q[rows, :].T.astype(BF16)
    copies[2].start()
    for copy in copies:
        copy.wait()


def shards(
    queries, keys, values, outputs, d_outputs, log_norm, rand_owner, rand_local, glob_blocks
):
    tokens, features = queries.shape
    heads = log_norm.shape[0]
    blocks = tokens // BLOCK
    many = glob_blocks.shape[0]
    owners = lax.axis_size("seq")
    references = blocks * rand_owner.shape[1]
    capacity = max(2, (references + owners - 1) // owners)
    by_permute = owners == 8
    whole = jax.ShapeDtypeStruct((tokens, features), BF16)
    wide = jax.ShapeDtypeStruct((tokens, features), F32)

    if by_permute:
        plan = [
            (capacity, (lambda me, k=k: ((me ^ k) == me + 1, (me ^ k) == me - 1)) if k in (1, 3, 7) else "xor")
            for k in range(owners)
        ]
    else:
        plan = [(capacity, None)] * owners
        plan.append((0, lambda me: (me < owners - 1, me < 0)))
        plan.append((0, lambda me: (me < 0, me > 0)))
    slots = [n + (edge not in (None, "xor")) for n, edge in plan]

    def in_hbm(*arrays):
        return [pltpu.with_memory_space_constraint(array, pltpu.HBM) for array in arrays]

    own = call(
        functools.partial(pick_globals, blocks),
        jax.ShapeDtypeStruct((2 * many * BLOCK, features), BF16),
        VMEM,
        [HBM] * 2 + [SMEM],
        [pltpu.SemaphoreType.DMA((2 * many,))],
        "pick_globals",
    )(*in_hbm(keys, values), glob_blocks)
    packed = call(
        lambda *refs: pack(heads, plan, refs),
        [
            whole,
            jax.ShapeDtypeStruct((blocks, STAT, BLOCK), F32),
            whole,
            jax.ShapeDtypeStruct((sum(slots),), jnp.int32),
        ]
        + [jax.ShapeDtypeStruct((message_rows(n), features), BF16) for n in slots],
        [VMEM] * 3 + [SMEM] + [VMEM] * len(plan),
        [HBM] * 7,
        [pltpu.VMEM((tokens, features), BF16)] * 4
        + [
            pltpu.VMEM(log_norm.shape, F32),
            pltpu.SMEM(rand_owner.shape[::-1], jnp.int32),
            pltpu.SMEM(rand_local.shape[::-1], jnp.int32),
            pltpu.SemaphoreType.DMA((7,)),
            pltpu.SMEM((owners,), jnp.int32),
            pltpu.SMEM((owners * capacity,), jnp.int32),
            pltpu.SMEM((owners * capacity,), jnp.int32),
        ],
        "pack",
    )(*in_hbm(queries, d_outputs, outputs, keys, log_norm, rand_owner.T, rand_local.T))
    scaled, stats, keys_t, source = packed[:4]
    outgoing = packed[4:]

    def swap(array, k):
        return lax.ppermute(array, "seq", [(i, i ^ k) for i in range(owners)])

    def add_globals(shared, dqt):
        return call(
            functools.partial(globals_, heads),
            [wide, jax.ShapeDtypeStruct(own.shape, BF16)],
            [VMEM] * 2,
            [VMEM] * 5,
            [pltpu.VMEM((many * BLOCK, features), F32)] * 2,
            "globals",
            {4: 0},
        )(scaled, d_outputs, stats, shared, dqt)

    def owned(taken, counts, dk, dv):
        shapes = [
            jax.ShapeDtypeStruct(a.shape[:-2] + (n * BLOCK, features), BF16) for a, n in zip(taken, counts)
        ]
        size = len(taken)
        outs = call(
            lambda *refs: randoms(heads, counts, refs),
            shapes + [wide, wide],
            [VMEM] * (size + 2),
            [VMEM] * (size + 5),
            [],
            "randoms",
            {size + 3: size, size + 4: size + 1},
        )(*taken, keys, values, keys_t, dk, dv)
        return outs[:size], outs[size], outs[size + 1]

    def add_window(stats):
        running = ()
        cuts = [blocks * n // PIECES for n in range(PIECES + 1)]
        for first, last in zip(cuts[:-1], cuts[1:]):
            running = call(
                functools.partial(window, heads, first, last),
                [wide] * 3,
                [VMEM] * 3,
                [VMEM] * (6 + len(running)),
                [],
                "window",
                {6 + n: n for n in range(len(running))},
            )(scaled, d_outputs, stats, keys, values, keys_t, *running)
        return running

    if by_permute:
        made = {}

        def gated(name, array):
            others = [get(other) for other in GATES.get(name, ())]
            return after(array, *[x if isinstance(x, jax.Array) else x[0] for x in others])

        def get(name):
            if name not in made:
                made[name] = None
                made[name] = make(name)
            if made[name] is None:
                raise ValueError("cycle")
            return made[name]

        def make(name):
            kind, number = name[0], int(name[1:] or 0)
            if kind == "F":
                return swap(gated(name, outgoing[number]), number) if number else outgoing[0]
            if kind == "G":
                if number == 0:
                    return own
                base = get(f"G{number - 1}")
                return base + swap(gated(name, base), HOPS["G"][number - 1])
            if kind == "P":
                if number == 0:
                    return get("g")[0]
                base = get(f"P{number - 1}")
                other = swap(gated(name, base), HOPS["P"][number - 1])
                return (base.astype(F32) + other.astype(F32)).astype(BF16)
            if kind == "W":
                return add_window(gated(name, stats))
            if kind == "g":
                return add_globals(gated(name, get("G3")), get("W")[0])[::-1]
            if kind == "R":
                before = get(f"R{number - 1}")[1:] if number else get("W")[1:]
                group = GROUPS[number]
                before = (gated(name, before[0]), before[1])
                return owned([get(f"F{k}") for k in group], [slots[k] for k in group], *before)
            if kind == "r":
                at = [n for n, group in enumerate(GROUPS) if number in group][0]
                back = get(f"R{at}")[0][GROUPS[at].index(number)]
                return swap(gated(name, back), number) if number else back

        rets = [get(f"r{k}") for k in range(owners)]
        _, dk, dv = get(f"R{len(GROUPS) - 1}")
        dqt = get("g")[1]
        part = get("P3")
        ret_slots = slots
    else:
        forward = [(i, i + 1) for i in range(owners - 1)]
        backward = [(j, i) for i, j in forward]
        everyone = lax.all_to_all(
            jnp.stack(outgoing[:owners]), "seq", split_axis=0, concat_axis=0, tiled=True
        )
        from_before = lax.ppermute(outgoing[owners], "seq", forward)
        from_after = lax.ppermute(outgoing[owners + 1], "seq", backward)
        shared = own
        step = 1
        while step < owners:
            shared = shared + swap(shared, step)
            step *= 2
        dqt, dk, dv = add_window(stats)
        dqt, part = add_globals(shared, dqt)
        step = 1
        while step < owners:
            part = (part.astype(F32) + swap(part, step).astype(F32)).astype(BF16)
            step *= 2
        backs, dk, dv = owned([everyone, from_before, from_after], [capacity, 1, 1], dk, dv)
        rets = [
            lax.all_to_all(backs[0], "seq", split_axis=0, concat_axis=0, tiled=True),
            lax.ppermute(backs[1], "seq", backward),
            lax.ppermute(backs[2], "seq", forward),
        ]
        ret_slots = [capacity, 1, 1]

    return call(
        lambda *refs: finish(ret_slots, refs),
        [whole] * 3,
        [HBM] * 3,
        [VMEM] * 4 + [HBM] * 2 + [VMEM] * len(rets),
        [pltpu.VMEM((tokens, features), F32)] * 3
        + [pltpu.VMEM((tokens, features), BF16)] * 3
        + [
            pltpu.SMEM(glob_blocks.shape, jnp.int32),
            pltpu.SMEM(source.shape, jnp.int32),
            pltpu.SemaphoreType.DMA((5,)),
        ],
        "finish",
    )(dqt, dk, dv, part, *in_hbm(glob_blocks, source), *rets)


def solution(mesh):
    placed = (
        P("seq", "head"),
        P("seq", "head"),
        P("seq", "head"),
        P("seq", "head"),
        P("seq", "head"),
        P("head", "seq"),
        P("seq", None),
        P("seq", None),
        P(),
    )
    return jax.shard_map(
        shards,
        mesh=mesh,
        in_specs=placed,
        out_specs=(P("seq", "head"), P("seq", "head"), P("seq", "head")),
        check_vma=False,
    )
```

```python
import functools
import math

import jax
import jax.numpy as jnp
from jax import lax
from jax.experimental import pallas as pl
from jax.experimental.pallas import tpu as pltpu
from jax.sharding import PartitionSpec as P

BLOCK = 128
STAT = 8
LOG2E = math.log2(math.e)
NT = (((1,), (1,)), ((), ()))
VMEM = pl.BlockSpec(memory_space=pltpu.VMEM)
SMEM = pl.BlockSpec(memory_space=pltpu.SMEM)
HBM = pl.BlockSpec(memory_space=pltpu.HBM)
F32 = jnp.float32
BF16 = jnp.bfloat16
LIMIT = 24
PIECES = 2
COSTS = {'window': 3, 'randoms': 3, 'finish': 3}
GATES = {'W': ['G1'], 'F5': ['G1'], 'F6': ['R0'], 'F7': ['F4'], 'F2': ['F5'], 'F3': ['F5'], 'R1': ['G2'], 'r6': ['r4'], 'r7': ['r5', 'F1', 'F6'], 'P2': ['F6', 'F7', 'r4'], 'P3': ['r5', 'F5'], 'r1': ['r6'], 'R0': ['G2'], 'G3': ['R1']}
GROUPS = [[4], [0], [5], [1], [2, 6], [7], [3]]
HOPS = {'G': [4, 2, 1], 'P': [1, 2, 4]}


def call(body, out_shape, out_specs, in_specs, scratch, name, aliases={}, limit=24):
    return pl.pallas_call(
        body,
        out_shape=out_shape,
        in_specs=in_specs,
        out_specs=out_specs,
        scratch_shapes=scratch,
        input_output_aliases=aliases,
        compiler_params=pltpu.CompilerParams(vmem_limit_bytes=int(limit * 1024 * 1024)),
        cost_estimate=pl.CostEstimate(
            flops=int(COSTS.get(name, 0) * 1.15e9), bytes_accessed=0, transcendentals=0
        ),
        name=name,
    )


def after(array, *others):
    return lax.optimization_barrier((array, *others))[0] if others else array


def dot(a, b):
    return jnp.dot(a, b, preferred_element_type=F32)


def by_head(rows, heads):
    width = rows.shape[1] // heads
    lane = lax.broadcasted_iota(jnp.int32, (1, rows.shape[1]), 1)
    parts = []
    for h in range(heads):
        keep = ((lane >= h * width) & (lane < (h + 1) * width)).astype(F32).astype(BF16)
        parts.append(rows * keep)
    return jnp.concatenate(parts, axis=0)


def stat_rows(tile, heads):
    half = 2 * heads
    norm = [tile[h : h + 1] + tile[heads + h : heads + h + 1] for h in range(heads)]
    delta = [tile[half + h : half + h + 1] + tile[half + heads + h : half + heads + h + 1] for h in range(heads)]
    return jnp.concatenate(norm, axis=1), jnp.concatenate(delta, axis=1)


def weigh(key_rows, value_rows, q_bd, g_bd, norm, delta):
    scores = lax.dot_general(key_rows, q_bd, NT, preferred_element_type=F32)
    weights = jnp.exp2(scores * LOG2E - norm)
    grad = lax.dot_general(value_rows, g_bd, NT, preferred_element_type=F32)
    return weights.astype(BF16), (weights * (grad - delta)).astype(BF16)


def grad_query_t(keys_t, low, heads):
    width = keys_t.shape[0] // heads
    return jnp.concatenate(
        [dot(keys_t[h * width : (h + 1) * width], low[:, h * BLOCK : (h + 1) * BLOCK]) for h in range(heads)],
        axis=0,
    )


def message_rows(slots):
    return -(-((2 * BLOCK + STAT + 1) * slots) // 16) * 16


def pick_globals(blocks, k_hbm, v_hbm, glob_hbm, own_ref, glob_ref, sems):
    many = glob_ref.shape[0]
    me = lax.axis_index("seq")
    names = pltpu.make_async_copy(glob_hbm, glob_ref, sems.at[2 * many])
    names.start()
    own_ref[...] = jnp.zeros_like(own_ref)
    names.wait()
    for waiting in (False, True):
        for number in range(many):
            block = glob_ref[number]

            @pl.when(block // blocks == me)
            def _():
                at = pl.ds(pl.multiple_of((block % blocks) * BLOCK, BLOCK), BLOCK)
                for turn, ref in enumerate((k_hbm, v_hbm)):
                    place = turn * many + number
                    copy = pltpu.make_async_copy(
                        ref.at[at, :], own_ref.at[pl.ds(place * BLOCK, BLOCK), :], sems.at[place]
                    )
                    copy.wait() if waiting else copy.start()


def pack(heads, plan, refs):
    q_hbm, g_hbm, o_hbm, k_hbm, norm_hbm, owner_hbm, local_hbm = refs[:7]
    scaled_ref, stats_ref, kt_ref, src_ref = refs[7:11]
    out_refs = refs[11 : 11 + len(plan)]
    q_ref, g_ref, o_ref, k_ref, norm_ref, owner_ref, local_ref, sems, count, source, place = refs[11 + len(plan) :]
    copies = [
        pltpu.make_async_copy(a, b, sems.at[n])
        for n, (a, b) in enumerate(
            (
                (owner_hbm, owner_ref),
                (local_hbm, local_ref),
                (g_hbm, g_ref),
                (o_hbm, o_ref),
                (norm_hbm, norm_ref),
                (q_hbm, q_ref),
                (k_hbm, k_ref),
            )
        )
    ]
    for copy in copies:
        copy.start()
    blocks = q_ref.shape[0] // BLOCK
    per_block = owner_ref.shape[0]
    width = q_ref.shape[1] // heads
    me = lax.axis_index("seq")
    fold = any(entry[1] == "xor" for entry in plan)
    most = max(entry[0] for entry in plan)
    randoms = sum(1 for entry in plan if entry[0])
    for copy in copies[:2]:
        copy.wait()
    for k in range(randoms):
        count[k] = 0
        for s in range(most):
            source[k * most + s] = -1
    for b in range(blocks):
        for r in range(per_block):
            k = owner_ref[r, b]
            if fold:
                k = k ^ me
            s = count[k]
            count[k] = s + 1
            source[k * most + s] = b
            place[k * most + s] = local_ref[r, b]
    for copy in copies[2:5]:
        copy.wait()
    for b in range(blocks):
        rows = pl.ds(b * BLOCK, BLOCK)
        prod = (o_ref[rows, :].astype(F32) * g_ref[rows, :].astype(F32)).T
        norm = [norm_ref[h : h + 1, rows] * LOG2E for h in range(heads)]
        delta = [jnp.sum(prod[h * width : (h + 1) * width], axis=0, keepdims=True) for h in range(heads)]
        exact = jnp.concatenate(norm + delta, axis=0)
        high = exact.astype(BF16).astype(F32)
        low = (exact - high).astype(BF16).astype(F32)
        stats_ref[b] = jnp.concatenate([high[:heads], low[:heads], high[heads:], low[heads:]], axis=0)
    copies[5].wait()
    scaled_ref[...] = q_ref[...] * jnp.asarray(1.0 / math.sqrt(width), BF16)
    full = blocks * per_block == randoms * most
    done = 0
    for k, (slots, edge) in enumerate(plan):
        out = out_refs[k]
        tiles, marks = [], []
        total = slots + (edge not in (None, "xor"))
        for s in range(total):
            if s < slots:
                b, number, sure = source[k * most + s], place[k * most + s], full
            else:
                up, down = edge(me)
                b = jnp.where(up, blocks - 1, jnp.where(down, 0, -1))
                number, sure = jnp.where(up, 0, blocks - 1), False
            src_ref[done + s] = b
            safe = jnp.maximum(b, 0)
            at = pl.ds(pl.multiple_of(safe * BLOCK, BLOCK), BLOCK)
            query, grad, tile = scaled_ref[at, :], g_ref[at, :], stats_ref[safe]
            if not sure:
                query = jnp.where(b >= 0, query, jnp.zeros_like(query))
                grad = jnp.where(b >= 0, grad, jnp.zeros_like(grad))
                tile = jnp.where(b >= 0, tile, jnp.zeros_like(tile))
                number = jnp.where(b >= 0, number, 0)
            out[2 * s * BLOCK : (2 * s + 1) * BLOCK, :] = query
            out[(2 * s + 1) * BLOCK : (2 * s + 2) * BLOCK, :] = grad
            tiles.append(tile)
            marks.append(jnp.full((1, BLOCK), number, jnp.int32).astype(F32))
        done += total
        extra = out.shape[0] - (2 * BLOCK + STAT + 1) * total
        if extra:
            marks.append(jnp.zeros((extra, BLOCK), F32))
        out[2 * total * BLOCK :, :] = jnp.concatenate(tiles + marks, axis=0).astype(BF16)
    copies[6].wait()
    for b in range(blocks):
        rows = pl.ds(b * BLOCK, BLOCK)
        kt_ref[rows, :] = (k_ref[rows, :].astype(F32) * (1.0 / math.sqrt(width))).T.astype(BF16)


def window(heads, first, last, q_ref, g_ref, stats_ref, k_ref, v_ref, kt_ref, *rest):
    dqt_ref, dk_ref, dv_ref = rest[-3:]
    blocks = q_ref.shape[0] // BLOCK
    if first == 0:
        dk_ref[...] = jnp.zeros_like(dk_ref)
        dv_ref[...] = jnp.zeros_like(dv_ref)
    for b in range(first, last):
        rows = pl.ds(b * BLOCK, BLOCK)
        q_bd, g_bd = by_head(q_ref[rows, :], heads), by_head(g_ref[rows, :], heads)
        norm, delta = stat_rows(stats_ref[b], heads)
        total = None
        for j in range(max(b - 1, 0), min(b + 2, blocks)):
            at = pl.ds(j * BLOCK, BLOCK)
            weights_low, scores_low = weigh(k_ref[at, :], v_ref[at, :], q_bd, g_bd, norm, delta)
            term = grad_query_t(kt_ref[at, :], scores_low, heads)
            total = term if total is None else total + term
            dk_ref[at, :] += dot(scores_low, q_bd)
            dv_ref[at, :] += dot(weights_low, g_bd)
        dqt_ref[rows, :] = total


def globals_(heads, q_ref, g_ref, stats_ref, shared_ref, _, dqt_ref, part_ref, total_k, total_v):
    blocks = q_ref.shape[0] // BLOCK
    head_size = q_ref.shape[1] // heads
    rows = shared_ref.shape[0] // 2
    key_rows, value_rows = shared_ref[:rows, :], shared_ref[rows:, :]
    keys_t = (key_rows.astype(F32) * (1.0 / math.sqrt(head_size))).T.astype(BF16)
    for b in range(blocks):
        at = pl.ds(b * BLOCK, BLOCK)
        q_bd, g_bd = by_head(q_ref[at, :], heads), by_head(g_ref[at, :], heads)
        norm, delta = stat_rows(stats_ref[b], heads)
        weights_low, scores_low = weigh(key_rows, value_rows, q_bd, g_bd, norm, delta)
        dqt_ref[at, :] += grad_query_t(keys_t, scores_low, heads)
        grad_key, grad_value = dot(scores_low, q_bd), dot(weights_low, g_bd)
        if b == 0:
            total_k[...] = grad_key
            total_v[...] = grad_value
        else:
            total_k[...] += grad_key
            total_v[...] += grad_value
    part_ref[:rows, :] = total_k[...].astype(BF16)
    part_ref[rows:, :] = total_v[...].astype(BF16)


def randoms(heads, slots, refs):
    many = len(slots)
    in_refs, (k_ref, v_ref, kt_ref) = refs[:many], refs[many : many + 3]
    ret_refs, (dk_ref, dv_ref) = refs[many + 5 : 2 * many + 5], refs[2 * many + 5 :]

    def partner(in_ref, ret_ref, total):
        tail = in_ref[2 * total * BLOCK :, :].astype(F32)
        for s in range(total):
            mark = STAT * total + s
            number = jnp.max(tail[mark : mark + 1]).astype(jnp.int32)
            at = pl.ds(pl.multiple_of(number * BLOCK, BLOCK), BLOCK)
            query = in_ref[2 * s * BLOCK : (2 * s + 1) * BLOCK, :]
            grad = in_ref[(2 * s + 1) * BLOCK : (2 * s + 2) * BLOCK, :]
            q_bd, g_bd = by_head(query, heads), by_head(grad, heads)
            norm, delta = stat_rows(tail[s * STAT : (s + 1) * STAT], heads)
            weights_low, scores_low = weigh(k_ref[at, :], v_ref[at, :], q_bd, g_bd, norm, delta)
            ret_ref[s * BLOCK : (s + 1) * BLOCK, :] = grad_query_t(kt_ref[at, :], scores_low, heads).astype(BF16)
            dk_ref[at, :] += dot(scores_low, q_bd)
            dv_ref[at, :] += dot(weights_low, g_bd)

    for in_ref, ret_ref, total in zip(in_refs, ret_refs, slots):
        if len(in_ref.shape) == 2:
            partner(in_ref, ret_ref, total)
        else:
            pl.loop(0, in_ref.shape[0])(lambda n, a=in_ref, b=ret_ref, c=total: partner(a.at[n], b.at[n], c))


def finish(slots, refs):
    dqt_ref, dk_in, dv_in, total_ref, glob_hbm, src_hbm = refs[:6]
    ret_refs = refs[6 : 6 + len(slots)]
    q_hbm, k_hbm, v_hbm, sum_q, sum_k, sum_v, q_out, k_out, v_out, glob_ref, src_ref, sems = refs[6 + len(slots) :]
    blocks = dk_in.shape[0] // BLOCK
    many = glob_ref.shape[0]
    me = lax.axis_index("seq")
    names = [
        pltpu.make_async_copy(a, b, sems.at[n]) for n, (a, b) in enumerate(((glob_hbm, glob_ref), (src_hbm, src_ref)))
    ]
    for copy in names:
        copy.start()
    sum_k[...] = dk_in[...]
    sum_v[...] = dv_in[...]
    sum_q[...] = dqt_ref[...]
    for copy in names:
        copy.wait()
    for number in range(many):
        block = glob_ref[number]

        @pl.when(block // blocks == me)
        def _():
            at = pl.ds(pl.multiple_of((block % blocks) * BLOCK, BLOCK), BLOCK)
            for turn, ref in enumerate((sum_k, sum_v)):
                first = (turn * many + number) * BLOCK
                ref[at, :] += total_ref[first : first + BLOCK, :].astype(F32)

    k_out[...] = sum_k[...].astype(BF16)
    v_out[...] = sum_v[...].astype(BF16)
    copies = [
        pltpu.make_async_copy(a, b, sems.at[2 + n])
        for n, (a, b) in enumerate(((k_out, k_hbm), (v_out, v_hbm), (q_out, q_hbm)))
    ]
    copies[0].start()
    copies[1].start()
    done = 0
    for ref, many_slots in zip(ret_refs, slots):
        parts = [ref] if len(ref.shape) == 2 else [ref.at[n] for n in range(ref.shape[0])]
        for part in parts:
            for s in range(many_slots):
                b = src_ref[done]
                done += 1

                @pl.when(b >= 0)
                def _():
                    rows = pl.ds(pl.multiple_of(b * BLOCK, BLOCK), BLOCK)
                    sum_q[rows, :] += part[s * BLOCK : (s + 1) * BLOCK, :].astype(F32)

    for b in range(blocks):
        rows = pl.ds(b * BLOCK, BLOCK)
        q_out[rows, :] = sum_q[rows, :].T.astype(BF16)
    copies[2].start()
    for copy in copies:
        copy.wait()


def shards(
    queries, keys, values, outputs, d_outputs, log_norm, rand_owner, rand_local, glob_blocks
):
    tokens, features = queries.shape
    heads = log_norm.shape[0]
    blocks = tokens // BLOCK
    many = glob_blocks.shape[0]
    owners = lax.axis_size("seq")
    references = blocks * rand_owner.shape[1]
    capacity = max(2, (references + owners - 1) // owners)
    by_permute = owners == 8
    whole = jax.ShapeDtypeStruct((tokens, features), BF16)
    wide = jax.ShapeDtypeStruct((tokens, features), F32)

    if by_permute:
        plan = [
            (capacity, (lambda me, k=k: ((me ^ k) == me + 1, (me ^ k) == me - 1)) if k in (1, 3, 7) else "xor")
            for k in range(owners)
        ]
    else:
        plan = [(capacity, None)] * owners
        plan.append((0, lambda me: (me < owners - 1, me < 0)))
        plan.append((0, lambda me: (me < 0, me > 0)))
    slots = [n + (edge not in (None, "xor")) for n, edge in plan]

    def in_hbm(*arrays):
        return [pltpu.with_memory_space_constraint(array, pltpu.HBM) for array in arrays]

    own = call(
        functools.partial(pick_globals, blocks),
        jax.ShapeDtypeStruct((2 * many * BLOCK, features), BF16),
        VMEM,
        [HBM] * 3,
        [pltpu.SMEM(glob_blocks.shape, jnp.int32), pltpu.SemaphoreType.DMA((2 * many + 1,))],
        "pick_globals",
    )(*in_hbm(keys, values, glob_blocks))
    packed = call(
        lambda *refs: pack(heads, plan, refs),
        [
            whole,
            jax.ShapeDtypeStruct((blocks, STAT, BLOCK), F32),
            whole,
            jax.ShapeDtypeStruct((sum(slots),), jnp.int32),
        ]
        + [jax.ShapeDtypeStruct((message_rows(n), features), BF16) for n in slots],
        [VMEM] * 3 + [SMEM] + [VMEM] * len(plan),
        [HBM] * 7,
        [pltpu.VMEM((tokens, features), BF16)] * 4
        + [
            pltpu.VMEM(log_norm.shape, F32),
            pltpu.SMEM(rand_owner.shape[::-1], jnp.int32),
            pltpu.SMEM(rand_local.shape[::-1], jnp.int32),
            pltpu.SemaphoreType.DMA((7,)),
            pltpu.SMEM((owners,), jnp.int32),
            pltpu.SMEM((owners * capacity,), jnp.int32),
            pltpu.SMEM((owners * capacity,), jnp.int32),
        ],
        "pack",
    )(*in_hbm(queries, d_outputs, outputs, keys, log_norm, rand_owner.T, rand_local.T))
    scaled, stats, keys_t, source = packed[:4]
    outgoing = packed[4:]

    def swap(array, k):
        return lax.ppermute(array, "seq", [(i, i ^ k) for i in range(owners)])

    def add_globals(shared, dqt):
        return call(
            functools.partial(globals_, heads),
            [wide, jax.ShapeDtypeStruct(own.shape, BF16)],
            [VMEM] * 2,
            [VMEM] * 5,
            [pltpu.VMEM((many * BLOCK, features), F32)] * 2,
            "globals",
            {4: 0},
        )(scaled, d_outputs, stats, shared, dqt)

    def owned(taken, counts, dk, dv):
        shapes = [
            jax.ShapeDtypeStruct(a.shape[:-2] + (n * BLOCK, features), BF16) for a, n in zip(taken, counts)
        ]
        size = len(taken)
        outs = call(
            lambda *refs: randoms(heads, counts, refs),
            shapes + [wide, wide],
            [VMEM] * (size + 2),
            [VMEM] * (size + 5),
            [],
            "randoms",
            {size + 3: size, size + 4: size + 1},
        )(*taken, keys, values, keys_t, dk, dv)
        return outs[:size], outs[size], outs[size + 1]

    def add_window(stats):
        running = ()
        cuts = [blocks * n // PIECES for n in range(PIECES + 1)]
        for first, last in zip(cuts[:-1], cuts[1:]):
            running = call(
                functools.partial(window, heads, first, last),
                [wide] * 3,
                [VMEM] * 3,
                [VMEM] * (6 + len(running)),
                [],
                "window",
                {6 + n: n for n in range(len(running))},
            )(scaled, d_outputs, stats, keys, values, keys_t, *running)
        return running

    if by_permute:
        made = {}

        def gated(name, array):
            others = [get(other) for other in GATES.get(name, ())]
            return after(array, *[x if isinstance(x, jax.Array) else x[0] for x in others])

        def get(name):
            if name not in made:
                made[name] = None
                made[name] = make(name)
            if made[name] is None:
                raise ValueError("cycle")
            return made[name]

        def make(name):
            kind, number = name[0], int(name[1:] or 0)
            if kind == "F":
                return swap(gated(name, outgoing[number]), number) if number else outgoing[0]
            if kind == "G":
                if number == 0:
                    return own
                base = get(f"G{number - 1}")
                return base + swap(gated(name, base), HOPS["G"][number - 1])
            if kind == "P":
                if number == 0:
                    return get("g")[0]
                base = get(f"P{number - 1}")
                other = swap(gated(name, base), HOPS["P"][number - 1])
                return (base.astype(F32) + other.astype(F32)).astype(BF16)
            if kind == "W":
                return add_window(gated(name, stats))
            if kind == "g":
                return add_globals(gated(name, get("G3")), get("W")[0])[::-1]
            if kind == "R":
                before = get(f"R{number - 1}")[1:] if number else get("W")[1:]
                group = GROUPS[number]
                before = (gated(name, before[0]), before[1])
                return owned([get(f"F{k}") for k in group], [slots[k] for k in group], *before)
            if kind == "r":
                at = [n for n, group in enumerate(GROUPS) if number in group][0]
                back = get(f"R{at}")[0][GROUPS[at].index(number)]
                return swap(gated(name, back), number) if number else back

        rets = [get(f"r{k}") for k in range(owners)]
        _, dk, dv = get(f"R{len(GROUPS) - 1}")
        dqt = get("g")[1]
        part = get("P3")
        ret_slots = slots
    else:
        forward = [(i, i + 1) for i in range(owners - 1)]
        backward = [(j, i) for i, j in forward]
        everyone = lax.all_to_all(
            jnp.stack(outgoing[:owners]), "seq", split_axis=0, concat_axis=0, tiled=True
        )
        from_before = lax.ppermute(outgoing[owners], "seq", forward)
        from_after = lax.ppermute(outgoing[owners + 1], "seq", backward)
        shared = own
        step = 1
        while step < owners:
            shared = shared + swap(shared, step)
            step *= 2
        dqt, dk, dv = add_window(stats)
        dqt, part = add_globals(shared, dqt)
        step = 1
        while step < owners:
            part = (part.astype(F32) + swap(part, step).astype(F32)).astype(BF16)
            step *= 2
        backs, dk, dv = owned([everyone, from_before, from_after], [capacity, 1, 1], dk, dv)
        rets = [
            lax.all_to_all(backs[0], "seq", split_axis=0, concat_axis=0, tiled=True),
            lax.ppermute(backs[1], "seq", backward),
            lax.ppermute(backs[2], "seq", forward),
        ]
        ret_slots = [capacity, 1, 1]

    return call(
        lambda *refs: finish(ret_slots, refs),
        [whole] * 3,
        [HBM] * 3,
        [VMEM] * 4 + [HBM] * 2 + [VMEM] * len(rets),
        [pltpu.VMEM((tokens, features), F32)] * 3
        + [pltpu.VMEM((tokens, features), BF16)] * 3
        + [
            pltpu.SMEM(glob_blocks.shape, jnp.int32),
            pltpu.SMEM(source.shape, jnp.int32),
            pltpu.SemaphoreType.DMA((5,)),
        ],
        "finish",
    )(dqt, dk, dv, part, *in_hbm(glob_blocks, source), *rets)


def solution(mesh):
    placed = (
        P("seq", "head"),
        P("seq", "head"),
        P("seq", "head"),
        P("seq", "head"),
        P("seq", "head"),
        P("head", "seq"),
        P("seq", None),
        P("seq", None),
        P(),
    )
    return jax.shard_map(
        shards,
        mesh=mesh,
        in_specs=placed,
        out_specs=(P("seq", "head"), P("seq", "head"), P("seq", "head")),
        check_vma=False,
    )
```

```python
import functools
import math

import jax
import jax.numpy as jnp
from jax import lax
from jax.experimental import pallas as pl
from jax.experimental.pallas import tpu as pltpu
from jax.sharding import PartitionSpec as P

BLOCK = 128
STAT = 8
LOG2E = math.log2(math.e)
NT = (((1,), (1,)), ((), ()))
VMEM = pl.BlockSpec(memory_space=pltpu.VMEM)
SMEM = pl.BlockSpec(memory_space=pltpu.SMEM)
HBM = pl.BlockSpec(memory_space=pltpu.HBM)
F32 = jnp.float32
BF16 = jnp.bfloat16
LIMIT = 24
PIECES = 2
COSTS = {'window': 3, 'randoms': 3, 'finish': 3}
GATES = {'W': ['G1'], 'F5': ['G1'], 'F6': ['R0'], 'F7': ['F4'], 'F2': ['F5'], 'F3': ['F5'], 'R1': ['G2'], 'r6': ['r4'], 'r7': ['r5', 'F1', 'F6'], 'P2': ['F6', 'F7', 'r4'], 'P3': ['r5', 'F5'], 'r1': ['r6'], 'R0': ['G2'], 'G3': ['R1']}
GROUPS = [[4], [0], [5], [1], [2, 6], [7], [3]]
HOPS = {'G': [4, 2, 1], 'P': [1, 2, 4]}


def call(body, out_shape, out_specs, in_specs, scratch, name, aliases={}, limit=24):
    return pl.pallas_call(
        body,
        out_shape=out_shape,
        in_specs=in_specs,
        out_specs=out_specs,
        scratch_shapes=scratch,
        input_output_aliases=aliases,
        compiler_params=pltpu.CompilerParams(vmem_limit_bytes=int(limit * 1024 * 1024)),
        cost_estimate=pl.CostEstimate(
            flops=int(COSTS.get(name, 0) * 1.15e9), bytes_accessed=0, transcendentals=0
        ),
        name=name,
    )


def after(array, *others):
    return lax.optimization_barrier((array, *others))[0] if others else array


def dot(a, b):
    return jnp.dot(a, b, preferred_element_type=F32)


def by_head(rows, heads):
    width = rows.shape[1] // heads
    lane = lax.broadcasted_iota(jnp.int32, (1, rows.shape[1]), 1)
    parts = []
    for h in range(heads):
        keep = ((lane >= h * width) & (lane < (h + 1) * width)).astype(F32).astype(BF16)
        parts.append(rows * keep)
    return jnp.concatenate(parts, axis=0)


def stat_rows(tile, heads):
    half = 2 * heads
    norm = [tile[h : h + 1] + tile[heads + h : heads + h + 1] for h in range(heads)]
    delta = [tile[half + h : half + h + 1] + tile[half + heads + h : half + heads + h + 1] for h in range(heads)]
    return jnp.concatenate(norm, axis=1), jnp.concatenate(delta, axis=1)


def weigh(key_rows, value_rows, q_bd, g_bd, norm, delta):
    scores = lax.dot_general(key_rows, q_bd, NT, preferred_element_type=F32)
    weights = jnp.exp2(scores * LOG2E - norm)
    grad = lax.dot_general(value_rows, g_bd, NT, preferred_element_type=F32)
    return weights.astype(BF16), (weights * (grad - delta)).astype(BF16)


def grad_query_t(keys_t, low, heads):
    width = keys_t.shape[0] // heads
    return jnp.concatenate(
        [dot(keys_t[h * width : (h + 1) * width], low[:, h * BLOCK : (h + 1) * BLOCK]) for h in range(heads)],
        axis=0,
    )


def message_rows(slots):
    return -(-((2 * BLOCK + STAT + 1) * slots) // 16) * 16


def pick_globals(blocks, k_hbm, v_hbm, glob_hbm, own_ref, glob_ref, sems):
    many = glob_ref.shape[0]
    me = lax.axis_index("seq")
    names = pltpu.make_async_copy(glob_hbm, glob_ref, sems.at[2 * many])
    names.start()
    own_ref[...] = jnp.zeros_like(own_ref)
    names.wait()
    for waiting in (False, True):
        for number in range(many):
            block = glob_ref[number]

            @pl.when(block // blocks == me)
            def _():
                at = pl.ds(pl.multiple_of((block % blocks) * BLOCK, BLOCK), BLOCK)
                for turn, ref in enumerate((k_hbm, v_hbm)):
                    place = turn * many + number
                    copy = pltpu.make_async_copy(
                        ref.at[at, :], own_ref.at[pl.ds(place * BLOCK, BLOCK), :], sems.at[place]
                    )
                    copy.wait() if waiting else copy.start()


def pack(heads, plan, refs):
    q_hbm, g_hbm, o_hbm, k_hbm, norm_hbm, owner_hbm, local_hbm = refs[:7]
    scaled_ref, stats_ref, kt_ref, src_hbm = refs[7:11]
    out_refs = refs[11 : 11 + len(plan)]
    q_ref, g_ref, o_ref, k_ref, norm_ref, owner_ref, local_ref, sems, count, source, place, src_ref = refs[
        11 + len(plan) :
    ]
    copies = [
        pltpu.make_async_copy(a, b, sems.at[n])
        for n, (a, b) in enumerate(
            (
                (owner_hbm, owner_ref),
                (local_hbm, local_ref),
                (g_hbm, g_ref),
                (o_hbm, o_ref),
                (norm_hbm, norm_ref),
                (q_hbm, q_ref),
                (k_hbm, k_ref),
            )
        )
    ]
    for copy in copies:
        copy.start()
    blocks = q_ref.shape[0] // BLOCK
    per_block = owner_ref.shape[0]
    width = q_ref.shape[1] // heads
    me = lax.axis_index("seq")
    fold = any(entry[1] == "xor" for entry in plan)
    most = max(entry[0] for entry in plan)
    randoms = sum(1 for entry in plan if entry[0])
    for copy in copies[:2]:
        copy.wait()
    for k in range(randoms):
        count[k] = 0
        for s in range(most):
            source[k * most + s] = -1
    for b in range(blocks):
        for r in range(per_block):
            k = owner_ref[r, b]
            if fold:
                k = k ^ me
            s = count[k]
            count[k] = s + 1
            source[k * most + s] = b
            place[k * most + s] = local_ref[r, b]
    for copy in copies[2:5]:
        copy.wait()
    for b in range(blocks):
        rows = pl.ds(b * BLOCK, BLOCK)
        prod = (o_ref[rows, :].astype(F32) * g_ref[rows, :].astype(F32)).T
        norm = [norm_ref[h : h + 1, rows] * LOG2E for h in range(heads)]
        delta = [jnp.sum(prod[h * width : (h + 1) * width], axis=0, keepdims=True) for h in range(heads)]
        exact = jnp.concatenate(norm + delta, axis=0)
        high = exact.astype(BF16).astype(F32)
        low = (exact - high).astype(BF16).astype(F32)
        stats_ref[b] = jnp.concatenate([high[:heads], low[:heads], high[heads:], low[heads:]], axis=0)
    copies[5].wait()
    scaled_ref[...] = q_ref[...] * jnp.asarray(1.0 / math.sqrt(width), BF16)
    full = blocks * per_block == randoms * most
    done = 0
    for k, (slots, edge) in enumerate(plan):
        out = out_refs[k]
        tiles, marks = [], []
        total = slots + (edge not in (None, "xor"))
        for s in range(total):
            if s < slots:
                b, number, sure = source[k * most + s], place[k * most + s], full
            else:
                up, down = edge(me)
                b = jnp.where(up, blocks - 1, jnp.where(down, 0, -1))
                number, sure = jnp.where(up, 0, blocks - 1), False
            src_ref[done + s] = b
            safe = jnp.maximum(b, 0)
            at = pl.ds(pl.multiple_of(safe * BLOCK, BLOCK), BLOCK)
            query, grad, tile = scaled_ref[at, :], g_ref[at, :], stats_ref[safe]
            if not sure:
                query = jnp.where(b >= 0, query, jnp.zeros_like(query))
                grad = jnp.where(b >= 0, grad, jnp.zeros_like(grad))
                tile = jnp.where(b >= 0, tile, jnp.zeros_like(tile))
                number = jnp.where(b >= 0, number, 0)
            out[2 * s * BLOCK : (2 * s + 1) * BLOCK, :] = query
            out[(2 * s + 1) * BLOCK : (2 * s + 2) * BLOCK, :] = grad
            tiles.append(tile)
            marks.append(jnp.full((1, BLOCK), number, jnp.int32).astype(F32))
        done += total
        extra = out.shape[0] - (2 * BLOCK + STAT + 1) * total
        if extra:
            marks.append(jnp.zeros((extra, BLOCK), F32))
        out[2 * total * BLOCK :, :] = jnp.concatenate(tiles + marks, axis=0).astype(BF16)
    table = pltpu.make_async_copy(src_ref, src_hbm, sems.at[7])
    table.start()
    copies[6].wait()
    for b in range(blocks):
        rows = pl.ds(b * BLOCK, BLOCK)
        kt_ref[rows, :] = (k_ref[rows, :].astype(F32) * (1.0 / math.sqrt(width))).T.astype(BF16)
    table.wait()


def window(heads, first, last, q_ref, g_ref, stats_ref, k_ref, v_ref, kt_ref, *rest):
    dqt_ref, dk_ref, dv_ref = rest[-3:]
    blocks = q_ref.shape[0] // BLOCK
    if first == 0:
        dk_ref[...] = jnp.zeros_like(dk_ref)
        dv_ref[...] = jnp.zeros_like(dv_ref)
    for b in range(first, last):
        rows = pl.ds(b * BLOCK, BLOCK)
        q_bd, g_bd = by_head(q_ref[rows, :], heads), by_head(g_ref[rows, :], heads)
        norm, delta = stat_rows(stats_ref[b], heads)
        total = None
        for j in range(max(b - 1, 0), min(b + 2, blocks)):
            at = pl.ds(j * BLOCK, BLOCK)
            weights_low, scores_low = weigh(k_ref[at, :], v_ref[at, :], q_bd, g_bd, norm, delta)
            term = grad_query_t(kt_ref[at, :], scores_low, heads)
            total = term if total is None else total + term
            dk_ref[at, :] += dot(scores_low, q_bd)
            dv_ref[at, :] += dot(weights_low, g_bd)
        dqt_ref[rows, :] = total


def globals_(heads, q_ref, g_ref, stats_ref, shared_ref, _, dqt_ref, part_ref, total_k, total_v):
    blocks = q_ref.shape[0] // BLOCK
    head_size = q_ref.shape[1] // heads
    rows = shared_ref.shape[0] // 2
    key_rows, value_rows = shared_ref[:rows, :], shared_ref[rows:, :]
    keys_t = (key_rows.astype(F32) * (1.0 / math.sqrt(head_size))).T.astype(BF16)
    for b in range(blocks):
        at = pl.ds(b * BLOCK, BLOCK)
        q_bd, g_bd = by_head(q_ref[at, :], heads), by_head(g_ref[at, :], heads)
        norm, delta = stat_rows(stats_ref[b], heads)
        weights_low, scores_low = weigh(key_rows, value_rows, q_bd, g_bd, norm, delta)
        dqt_ref[at, :] += grad_query_t(keys_t, scores_low, heads)
        grad_key, grad_value = dot(scores_low, q_bd), dot(weights_low, g_bd)
        if b == 0:
            total_k[...] = grad_key
            total_v[...] = grad_value
        else:
            total_k[...] += grad_key
            total_v[...] += grad_value
    part_ref[:rows, :] = total_k[...].astype(BF16)
    part_ref[rows:, :] = total_v[...].astype(BF16)


def randoms(heads, slots, refs):
    many = len(slots)
    in_refs, (k_ref, v_ref, kt_ref) = refs[:many], refs[many : many + 3]
    ret_refs, (dk_ref, dv_ref) = refs[many + 5 : 2 * many + 5], refs[2 * many + 5 :]

    def partner(in_ref, ret_ref, total):
        tail = in_ref[2 * total * BLOCK :, :].astype(F32)
        for s in range(total):
            mark = STAT * total + s
            number = jnp.max(tail[mark : mark + 1]).astype(jnp.int32)
            at = pl.ds(pl.multiple_of(number * BLOCK, BLOCK), BLOCK)
            query = in_ref[2 * s * BLOCK : (2 * s + 1) * BLOCK, :]
            grad = in_ref[(2 * s + 1) * BLOCK : (2 * s + 2) * BLOCK, :]
            q_bd, g_bd = by_head(query, heads), by_head(grad, heads)
            norm, delta = stat_rows(tail[s * STAT : (s + 1) * STAT], heads)
            weights_low, scores_low = weigh(k_ref[at, :], v_ref[at, :], q_bd, g_bd, norm, delta)
            ret_ref[s * BLOCK : (s + 1) * BLOCK, :] = grad_query_t(kt_ref[at, :], scores_low, heads).astype(BF16)
            dk_ref[at, :] += dot(scores_low, q_bd)
            dv_ref[at, :] += dot(weights_low, g_bd)

    for in_ref, ret_ref, total in zip(in_refs, ret_refs, slots):
        if len(in_ref.shape) == 2:
            partner(in_ref, ret_ref, total)
        else:
            pl.loop(0, in_ref.shape[0])(lambda n, a=in_ref, b=ret_ref, c=total: partner(a.at[n], b.at[n], c))


def finish(slots, refs):
    dqt_ref, dk_in, dv_in, total_ref, glob_hbm, src_hbm = refs[:6]
    ret_refs = refs[6 : 6 + len(slots)]
    q_hbm, k_hbm, v_hbm, sum_q, sum_k, sum_v, q_out, k_out, v_out, glob_ref, src_ref, sems = refs[6 + len(slots) :]
    blocks = dk_in.shape[0] // BLOCK
    many = glob_ref.shape[0]
    me = lax.axis_index("seq")
    names = [
        pltpu.make_async_copy(a, b, sems.at[n]) for n, (a, b) in enumerate(((glob_hbm, glob_ref), (src_hbm, src_ref)))
    ]
    for copy in names:
        copy.start()
    sum_k[...] = dk_in[...]
    sum_v[...] = dv_in[...]
    sum_q[...] = dqt_ref[...]
    for copy in names:
        copy.wait()
    for number in range(many):
        block = glob_ref[number]

        @pl.when(block // blocks == me)
        def _():
            at = pl.ds(pl.multiple_of((block % blocks) * BLOCK, BLOCK), BLOCK)
            for turn, ref in enumerate((sum_k, sum_v)):
                first = (turn * many + number) * BLOCK
                ref[at, :] += total_ref[first : first + BLOCK, :].astype(F32)

    k_out[...] = sum_k[...].astype(BF16)
    v_out[...] = sum_v[...].astype(BF16)
    copies = [
        pltpu.make_async_copy(a, b, sems.at[2 + n])
        for n, (a, b) in enumerate(((k_out, k_hbm), (v_out, v_hbm), (q_out, q_hbm)))
    ]
    copies[0].start()
    copies[1].start()
    done = 0
    for ref, many_slots in zip(ret_refs, slots):
        parts = [ref] if len(ref.shape) == 2 else [ref.at[n] for n in range(ref.shape[0])]
        for part in parts:
            for s in range(many_slots):
                b = src_ref[done]
                done += 1

                @pl.when(b >= 0)
                def _():
                    rows = pl.ds(pl.multiple_of(b * BLOCK, BLOCK), BLOCK)
                    sum_q[rows, :] += part[s * BLOCK : (s + 1) * BLOCK, :].astype(F32)

    for b in range(blocks):
        rows = pl.ds(b * BLOCK, BLOCK)
        q_out[rows, :] = sum_q[rows, :].T.astype(BF16)
    copies[2].start()
    for copy in copies:
        copy.wait()


def shards(
    queries, keys, values, outputs, d_outputs, log_norm, rand_owner, rand_local, glob_blocks
):
    tokens, features = queries.shape
    heads = log_norm.shape[0]
    blocks = tokens // BLOCK
    many = glob_blocks.shape[0]
    owners = lax.axis_size("seq")
    references = blocks * rand_owner.shape[1]
    capacity = max(2, (references + owners - 1) // owners)
    by_permute = owners == 8
    whole = jax.ShapeDtypeStruct((tokens, features), BF16)
    wide = jax.ShapeDtypeStruct((tokens, features), F32)

    if by_permute:
        plan = [
            (capacity, (lambda me, k=k: ((me ^ k) == me + 1, (me ^ k) == me - 1)) if k in (1, 3, 7) else "xor")
            for k in range(owners)
        ]
    else:
        plan = [(capacity, None)] * owners
        plan.append((0, lambda me: (me < owners - 1, me < 0)))
        plan.append((0, lambda me: (me < 0, me > 0)))
    slots = [n + (edge not in (None, "xor")) for n, edge in plan]

    def in_hbm(*arrays):
        return [pltpu.with_memory_space_constraint(array, pltpu.HBM) for array in arrays]

    own = call(
        functools.partial(pick_globals, blocks),
        jax.ShapeDtypeStruct((2 * many * BLOCK, features), BF16),
        VMEM,
        [HBM] * 3,
        [pltpu.SMEM(glob_blocks.shape, jnp.int32), pltpu.SemaphoreType.DMA((2 * many + 1,))],
        "pick_globals",
    )(*in_hbm(keys, values, glob_blocks))
    packed = call(
        lambda *refs: pack(heads, plan, refs),
        [
            whole,
            jax.ShapeDtypeStruct((blocks, STAT, BLOCK), F32),
            whole,
            pltpu.HBM((sum(slots),), jnp.int32),
        ]
        + [jax.ShapeDtypeStruct((message_rows(n), features), BF16) for n in slots],
        [VMEM] * 3 + [HBM] + [VMEM] * len(plan),
        [HBM] * 7,
        [pltpu.VMEM((tokens, features), BF16)] * 4
        + [
            pltpu.VMEM(log_norm.shape, F32),
            pltpu.SMEM(rand_owner.shape[::-1], jnp.int32),
            pltpu.SMEM(rand_local.shape[::-1], jnp.int32),
            pltpu.SemaphoreType.DMA((8,)),
            pltpu.SMEM((owners,), jnp.int32),
            pltpu.SMEM((owners * capacity,), jnp.int32),
            pltpu.SMEM((owners * capacity,), jnp.int32),
            pltpu.SMEM((sum(slots),), jnp.int32),
        ],
        "pack",
    )(*in_hbm(queries, d_outputs, outputs, keys, log_norm, rand_owner.T, rand_local.T))
    scaled, stats, keys_t, source = packed[:4]
    outgoing = packed[4:]

    def swap(array, k):
        return lax.ppermute(array, "seq", [(i, i ^ k) for i in range(owners)])

    def add_globals(shared, dqt):
        return call(
            functools.partial(globals_, heads),
            [wide, jax.ShapeDtypeStruct(own.shape, BF16)],
            [VMEM] * 2,
            [VMEM] * 5,
            [pltpu.VMEM((many * BLOCK, features), F32)] * 2,
            "globals",
            {4: 0},
        )(scaled, d_outputs, stats, shared, dqt)

    def owned(taken, counts, dk, dv):
        shapes = [
            jax.ShapeDtypeStruct(a.shape[:-2] + (n * BLOCK, features), BF16) for a, n in zip(taken, counts)
        ]
        size = len(taken)
        outs = call(
            lambda *refs: randoms(heads, counts, refs),
            shapes + [wide, wide],
            [VMEM] * (size + 2),
            [VMEM] * (size + 5),
            [],
            "randoms",
            {size + 3: size, size + 4: size + 1},
        )(*taken, keys, values, keys_t, dk, dv)
        return outs[:size], outs[size], outs[size + 1]

    def add_window(stats):
        running = ()
        cuts = [blocks * n // PIECES for n in range(PIECES + 1)]
        for first, last in zip(cuts[:-1], cuts[1:]):
            running = call(
                functools.partial(window, heads, first, last),
                [wide] * 3,
                [VMEM] * 3,
                [VMEM] * (6 + len(running)),
                [],
                "window",
                {6 + n: n for n in range(len(running))},
            )(scaled, d_outputs, stats, keys, values, keys_t, *running)
        return running

    if by_permute:
        made = {}

        def gated(name, array):
            others = [get(other) for other in GATES.get(name, ())]
            return after(array, *[x if isinstance(x, jax.Array) else x[0] for x in others])

        def get(name):
            if name not in made:
                made[name] = None
                made[name] = make(name)
            if made[name] is None:
                raise ValueError("cycle")
            return made[name]

        def make(name):
            kind, number = name[0], int(name[1:] or 0)
            if kind == "F":
                return swap(gated(name, outgoing[number]), number) if number else outgoing[0]
            if kind == "G":
                if number == 0:
                    return own
                base = get(f"G{number - 1}")
                return base + swap(gated(name, base), HOPS["G"][number - 1])
            if kind == "P":
                if number == 0:
                    return get("g")[0]
                base = get(f"P{number - 1}")
                other = swap(gated(name, base), HOPS["P"][number - 1])
                return (base.astype(F32) + other.astype(F32)).astype(BF16)
            if kind == "W":
                return add_window(gated(name, stats))
            if kind == "g":
                return add_globals(gated(name, get("G3")), get("W")[0])[::-1]
            if kind == "R":
                before = get(f"R{number - 1}")[1:] if number else get("W")[1:]
                group = GROUPS[number]
                before = (gated(name, before[0]), before[1])
                return owned([get(f"F{k}") for k in group], [slots[k] for k in group], *before)
            if kind == "r":
                at = [n for n, group in enumerate(GROUPS) if number in group][0]
                back = get(f"R{at}")[0][GROUPS[at].index(number)]
                return swap(gated(name, back), number) if number else back

        rets = [get(f"r{k}") for k in range(owners)]
        _, dk, dv = get(f"R{len(GROUPS) - 1}")
        dqt = get("g")[1]
        part = get("P3")
        ret_slots = slots
    else:
        forward = [(i, i + 1) for i in range(owners - 1)]
        backward = [(j, i) for i, j in forward]
        everyone = lax.all_to_all(
            jnp.stack(outgoing[:owners]), "seq", split_axis=0, concat_axis=0, tiled=True
        )
        from_before = lax.ppermute(outgoing[owners], "seq", forward)
        from_after = lax.ppermute(outgoing[owners + 1], "seq", backward)
        shared = own
        step = 1
        while step < owners:
            shared = shared + swap(shared, step)
            step *= 2
        dqt, dk, dv = add_window(stats)
        dqt, part = add_globals(shared, dqt)
        step = 1
        while step < owners:
            part = (part.astype(F32) + swap(part, step).astype(F32)).astype(BF16)
            step *= 2
        backs, dk, dv = owned([everyone, from_before, from_after], [capacity, 1, 1], dk, dv)
        rets = [
            lax.all_to_all(backs[0], "seq", split_axis=0, concat_axis=0, tiled=True),
            lax.ppermute(backs[1], "seq", backward),
            lax.ppermute(backs[2], "seq", forward),
        ]
        ret_slots = [capacity, 1, 1]

    return call(
        lambda *refs: finish(ret_slots, refs),
        [whole] * 3,
        [HBM] * 3,
        [VMEM] * 4 + [HBM] * 2 + [VMEM] * len(rets),
        [pltpu.VMEM((tokens, features), F32)] * 3
        + [pltpu.VMEM((tokens, features), BF16)] * 3
        + [
            pltpu.SMEM(glob_blocks.shape, jnp.int32),
            pltpu.SMEM(source.shape, jnp.int32),
            pltpu.SemaphoreType.DMA((5,)),
        ],
        "finish",
    )(dqt, dk, dv, part, *in_hbm(glob_blocks, source), *rets)


def solution(mesh):
    placed = (
        P("seq", "head"),
        P("seq", "head"),
        P("seq", "head"),
        P("seq", "head"),
        P("seq", "head"),
        P("head", "seq"),
        P("seq", None),
        P("seq", None),
        P(),
    )
    return jax.shard_map(
        shards,
        mesh=mesh,
        in_specs=placed,
        out_specs=(P("seq", "head"), P("seq", "head"), P("seq", "head")),
        check_vma=False,
    )
```
